32 devices in a mesh: blk: 4 (over y, x), sub: 2 (over core), feat: 4 (over z).
Axes of the slice: x: 2, y: 2, z: 4, core: 2. Of those that a mesh axis runs over, the one named last changes fastest.
Arguments:
- sources: bfloat16 [65536, 1024], P(('blk', 'sub'), 'feat'), may hold values from -6 to 6
- adjacency: bfloat16 [8, 8, 64, 128, 128], P(('blk', 'sub')), may hold values from -0.15625 to 0.15625
- target_block: int32 [8, 8, 64], P(('blk', 'sub')), may hold values from 0 to 7
- source_block: int32 [8, 8, 64], P(('blk', 'sub')), may hold values from 0 to 63
- slot_counts: int32 [8, 8], P(('blk', 'sub')), may hold values from 1 to 64, as said below
- weight: bfloat16 [1024, 1024], P(None, 'feat'), may hold values from -0.1875 to 0.1875
Outputs:
- activated: bfloat16 [8192, 1024], P(('blk', 'sub'), 'feat')
The draws below stay inside these ranges and needn't reach their ends.
Inputs may be any that keep to these rules, and one draw needn't show every extreme that they name: Every stripe and piece uses its first slot_counts slots; in every draw some stripe and piece uses all 64.
All inputs are finite; a program needn't handle non-finite values.
Results may differ from the reference program's by a relative error of at most 0.0049.
Values may be sent and summed in bfloat16 or wider, within the bound.
No kernel may reach another device: no remote copies, remote signals or barrier semaphores. Data moves between devices by JAX's collectives and lax.ppermute only.
A program may use at most 256 MiB of HBM per device.

```python
import jax
import jax.numpy as jnp
from jax import lax

F = 1024
BLOCK = 128
TGT_DEV = 1024
SRC_DEV = 8192
NSTRIPE = 8
SLOTS = 64
TGT = 8192
SRC = 65536


def draw_slot_counts(key, part):
    key_level = jax.random.fold_in(key, 11)
    key_count = jax.random.fold_in(key, 12)
    key_pick = jax.random.fold_in(key, 13)
    level = jnp.left_shift(jnp.int32(1), jax.random.randint(key_level, (NSTRIPE, 1), 0, 4))
    ceiling = jnp.maximum(1, SLOTS * level // 8)
    lowest = (ceiling + 1) // 2
    spread = jax.random.randint(key_count, (NSTRIPE, NSTRIPE), 0, 1 << 20)
    counts = lowest + spread % (ceiling - lowest + 1)
    picked = jax.random.randint(key_pick, (), 0, NSTRIPE * NSTRIPE)
    flat_counts = counts.reshape(-1).at[picked].set(SLOTS)
    return flat_counts.reshape(NSTRIPE, NSTRIPE).astype(jnp.int32)


def plant(result, stream_key, least, high):
    longest = result.shape.index(max(result.shape))
    spots = []
    for shift in (0, 1):
        where = [jax.random.randint(jax.random.fold_in(stream_key, axis), (), 0, length) for axis, length in enumerate(result.shape)]
        where[longest] = (where[longest] + shift) % result.shape[longest]
        spots.append(tuple(where))
    return result.at[spots[0]].set(least).at[spots[1]].set(high)


def spiked(entries, key, source, target, shards_of, factor):
    def block_of(dim):
        return (jnp.arange(entries.shape[dim]) // (entries.shape[dim] // shards_of)).reshape((-1,) + (1,) * (entries.ndim - 1 - dim))

    near = jax.random.permutation(key, shards_of)[block_of(target)]
    second = (block_of(target) + shards_of // 2) % shards_of
    return jnp.where((block_of(source) == near) | (block_of(source) == second), factor * entries, entries)


def levels(rng, dims, cuts, smallest, top_value):
    gain, own = 1.0, jax.random.fold_in(rng, 6)
    for dim, blocks in cuts:
        heights = jnp.exp(jax.random.uniform(jax.random.fold_in(own, dim), (blocks,), jnp.float32, smallest / len(cuts), top_value / len(cuts)))
        gain = gain * jnp.repeat(heights, dims[dim] // blocks).reshape([-1 if axis == dim else 1 for axis in range(len(dims))])
    return gain


def normal_values(own_key, extent, scale, reach, pieces=(), kind=jnp.bfloat16):
    values = scale * jax.random.normal(own_key, extent, jnp.float32)
    if pieces:
        values = values * levels(own_key, extent, pieces, -0.22, 0.18)
    return jnp.clip(values, -reach, reach).astype(kind)


def bell_draw_with(own_key, shape, scale, most, shards, heavy, kind=jnp.bfloat16):
    values = scale * jax.random.normal(own_key, shape, jnp.float32)
    if shards:
        values = values * levels(own_key, shape, shards, -0.22, 0.18)
    return jnp.clip(spiked(values, jax.random.fold_in(own_key, 3), *heavy), -most, most).astype(kind)


def setup_inputs(seed: int = 0) -> dict:
    key_list = jax.random.split(jax.random.key(seed), 7)
    sources = normal_values(key_list[0], (SRC, F), 1.0, 6.0, ((0, 8), (1, 4)))
    adjacency = bell_draw_with(key_list[1], (NSTRIPE, NSTRIPE, SLOTS, BLOCK, BLOCK), (NSTRIPE * SLOTS * BLOCK * BLOCK // (3 * TGT_DEV)) ** -0.5, 0.15625, ((0, 8),), (0, 1, 8, 2.0))
    target_block = plant(jax.random.randint(key_list[2], (NSTRIPE, NSTRIPE, SLOTS), 0, TGT_DEV // BLOCK), jax.random.fold_in(key_list[2], 1), 0, (TGT_DEV // BLOCK) - 1).astype(jnp.int32)
    source_block = plant(jax.random.randint(key_list[3], (NSTRIPE, NSTRIPE, SLOTS), 0, SRC_DEV // BLOCK), jax.random.fold_in(key_list[3], 1), 0, (SRC_DEV // BLOCK) - 1).astype(jnp.int32)
    slot_counts = draw_slot_counts(jax.random.fold_in(key_list[6], 71), 0)
    weight = normal_values(key_list[5], (F, F), F ** -0.5, 0.1875, ((1, 4),))
    return {"sources": sources, "adjacency": adjacency, "target_block": target_block, "source_block": source_block, "slot_counts": slot_counts, "weight": weight}


def reference(sources, adjacency, target_block, source_block, slot_counts, weight):
    blocks_all = sources.reshape(NSTRIPE, SRC_DEV // BLOCK, BLOCK, F)

    def add_stripe(running, packed):
        adj_stripe, rows_stripe, cols_stripe, counts_stripe, blocks = packed

        def one_piece(adj_piece, rows_piece, cols_piece, count_piece):
            gathered = blocks[cols_piece].astype(jnp.float32)
            product = jnp.einsum("sij,sjf->sif", adj_piece.astype(jnp.float32), gathered)
            live_mask = (jnp.arange(SLOTS) < count_piece).astype(jnp.float32)
            summed = jax.ops.segment_sum(product * live_mask[:, None, None], rows_piece, num_segments=TGT_DEV // BLOCK)
            return summed.reshape(TGT_DEV, F)

        return running + jax.vmap(one_piece)(adj_stripe, rows_stripe, cols_stripe, counts_stripe), None

    initial = jnp.zeros((NSTRIPE, TGT_DEV, F), jnp.float32)
    aggregated, _ = lax.scan(add_stripe, initial, (adjacency, target_block, source_block, slot_counts, blocks_all))
    hidden = aggregated.reshape(TGT, F).astype(jnp.bfloat16)
    projected = jnp.dot(hidden, weight, preferred_element_type=jnp.float32)
    return jax.nn.relu(projected).astype(jnp.bfloat16)
```

```python
import functools

import jax
import jax.numpy as jnp
from jax import lax
from jax.experimental import pallas as pl
from jax.experimental.pallas import tpu as pltpu
from jax.sharding import PartitionSpec as P

TGT_DEV = 1024
GROUP = 8
VMEM_BYTES = 48 * 2**20


def forward(index, step, size):
    if size & (size - 1) == 0:
        return index ^ step
    return (index + step) % size


def backward(index, step, size):
    if size & (size - 1) == 0:
        return index ^ step
    return (index + size - step) % size


def send(value, axis, step):
    size = lax.axis_size(axis)
    return lax.ppermute(value, axis, [(i, forward(i, step, size)) for i in range(size)])


def fetch(value, axis, step):
    size = lax.axis_size(axis)
    return lax.ppermute(value, axis, [(forward(i, step, size), i) for i in range(size)])


def products_kernel(target, source, count, ids, src_hbm, adj_hbm, out, src, adj, acc, src_sem, adj_sem):
    step = pl.program_id(0)
    pieces, slots, block, _ = adj.shape
    targets = acc.shape[0] - 1
    src_copy = pltpu.make_async_copy(src_hbm, src, src_sem)

    def tiles(piece, group):
        rows = pl.ds(group * GROUP, GROUP)
        return pltpu.make_async_copy(
            adj_hbm.at[ids[piece], rows], adj.at[piece, rows], adj_sem.at[piece, group]
        )

    def groups(piece):
        return (count[ids[piece]] + GROUP - 1) // GROUP

    @pl.when(step == 0)
    def _():
        src_copy.start()

        @pl.loop(0, pieces)
        def _(piece):
            @pl.loop(0, groups(piece))
            def _(group):
                tiles(piece, group).start()

        src_copy.wait()

    here = ids[step]
    acc[...] = jnp.zeros_like(acc)

    @pl.loop(0, groups(step))
    def _(group):
        tiles(step, group).wait()
        for lane in range(GROUP):
            slot = group * GROUP + lane
            row = jnp.where(slot < count[here], target[here, slot], targets)
            rows = pl.ds(pl.multiple_of(source[here, slot] * block, block), block)
            acc[row] += jnp.dot(adj[step, slot], src[rows, :], preferred_element_type=jnp.float32)

    for row in range(targets):
        out[0, row * block : (row + 1) * block, :] = acc[row].astype(out.dtype)


def products(sources, adjacency, target, source, count, ids):
    _, slots, block, _ = adjacency.shape
    pieces = ids.shape[0]
    feat = sources.shape[1]
    return pl.pallas_call(
        products_kernel,
        grid_spec=pltpu.PrefetchScalarGridSpec(
            num_scalar_prefetch=4,
            grid=(pieces,),
            in_specs=[pl.BlockSpec(memory_space=pl.ANY)] * 2,
            out_specs=pl.BlockSpec((1, TGT_DEV, feat), lambda step, *_: (step, 0, 0)),
            scratch_shapes=[
                pltpu.VMEM(sources.shape, sources.dtype),
                pltpu.VMEM((pieces, slots, block, block), adjacency.dtype),
                pltpu.VMEM((TGT_DEV // block + 1, block, feat), jnp.float32),
                pltpu.SemaphoreType.DMA,
                pltpu.SemaphoreType.DMA((pieces, slots // GROUP)),
            ],
        ),
        out_shape=jax.ShapeDtypeStruct((pieces, TGT_DEV, feat), jnp.bfloat16),
        compiler_params=pltpu.CompilerParams(vmem_limit_bytes=VMEM_BYTES),
        cost_estimate=pl.CostEstimate(
            flops=2 * pieces * slots * block * block * feat,
            bytes_accessed=2 * (sources.size + pieces * slots * block * block),
            transcendentals=0,
        ),
        name="products",
    )(target, source, count, ids, sources, adjacency)


def pair_sum_kernel(own, *refs):
    parts = own.shape[0]
    others, outs = refs[:-parts], refs[-parts:]
    for part in range(parts):
        total = own[part].astype(jnp.float32)
        for other in others:
            total += other[part].astype(jnp.float32)
        outs[part][...] = total.astype(outs[part].dtype)


def pair_sum(own, others):
    parts, rows, feat = own.shape
    tile = rows // 4
    return pl.pallas_call(
        pair_sum_kernel,
        grid=(rows // tile,),
        in_specs=[pl.BlockSpec((parts, tile, feat), lambda i: (0, i, 0))] * (1 + len(others)),
        out_specs=[pl.BlockSpec((tile, feat), lambda i: (i, 0))] * parts,
        out_shape=[
            jax.ShapeDtypeStruct((rows, feat), jnp.float32 if part == 0 else jnp.bfloat16)
            for part in range(parts)
        ],
        cost_estimate=pl.CostEstimate(
            flops=own.size * len(others), bytes_accessed=6 * own.size, transcendentals=0
        ),
        name="pair_sum",
    )(own, *others)


def deal_kernel(places, own, *refs):
    quarters = places.shape[0]
    others, outs = refs[:-quarters], refs[-quarters:]
    rows = outs[0].shape[0]
    for quarter in range(quarters):
        here = pl.ds(pl.multiple_of(places[quarter] * rows, rows), rows)
        total = own[here, :]
        for other in others:
            total += other[here, :].astype(jnp.float32)
        outs[quarter][...] = total.astype(jnp.bfloat16)


def deal(places, own, others):
    quarters = places.shape[0]
    rows, feat = own.shape
    vmem = pl.BlockSpec(memory_space=pltpu.VMEM)
    return pl.pallas_call(
        deal_kernel,
        in_specs=[pl.BlockSpec(memory_space=pltpu.SMEM)] + [vmem] * (1 + len(others)),
        out_specs=[vmem] * quarters,
        out_shape=[jax.ShapeDtypeStruct((rows // quarters, feat), jnp.bfloat16)] * quarters,
        cost_estimate=pl.CostEstimate(
            flops=own.size * len(others), bytes_accessed=10 * own.size, transcendentals=0
        ),
        name="deal",
    )(places, own, *others)


def layer_kernel(places, *refs):
    parts = places.shape[0]
    hidden, weights, outs = refs[:parts], refs[parts : 2 * parts], refs[2 * parts :]
    depth = hidden[0].shape[1]
    for part in range(parts):
        total = None
        for inner in range(parts):
            rows = pl.ds(pl.multiple_of(places[inner] * depth, depth), depth)
            term = jnp.dot(
                hidden[inner][...], weights[part][rows, :], preferred_element_type=jnp.float32
            )
            total = term if total is None else total + term
        outs[part][...] = jnp.maximum(total, 0.0).astype(outs[part].dtype)


def layer(places, hidden, weights):
    parts = len(hidden)
    rows = hidden[0].shape[0]
    depth, columns = weights[0].shape
    vmem = pl.BlockSpec(memory_space=pltpu.VMEM)
    return pl.pallas_call(
        layer_kernel,
        in_specs=[pl.BlockSpec(memory_space=pltpu.SMEM)] + [vmem] * (2 * parts),
        out_specs=[vmem] * parts,
        out_shape=[jax.ShapeDtypeStruct((rows, columns), jnp.bfloat16)] * parts,
        cost_estimate=pl.CostEstimate(
            flops=2 * rows * depth * columns * parts,
            bytes_accessed=2 * parts * depth * columns,
            transcendentals=0,
        ),
        name="layer",
    )(places, *hidden, *weights)


def gather_rows_kernel(places, *refs):
    out = refs[-1]
    for part, piece in enumerate(refs[:-1]):
        rows = piece.shape[0]
        out[pl.ds(pl.multiple_of(places[part] * rows, rows), rows), :] = piece[...]


def gather_rows(places, pieces):
    rows, columns = pieces[0].shape
    vmem = pl.BlockSpec(memory_space=pltpu.VMEM)
    return pl.pallas_call(
        gather_rows_kernel,
        in_specs=[pl.BlockSpec(memory_space=pltpu.SMEM)] + [vmem] * len(pieces),
        out_specs=vmem,
        out_shape=jax.ShapeDtypeStruct((rows * len(pieces), columns), pieces[0].dtype),
        name="gather_rows",
    )(places, *pieces)


def body(sources, adjacency, target_block, source_block, slot_counts, weight):
    blks, subs, feats = (lax.axis_size(axis) for axis in ("blk", "sub", "feat"))
    blk, sub, feat = (lax.axis_index(axis) for axis in ("blk", "sub", "feat"))

    def local(step):
        ids = jnp.stack(
            [forward(blk, part, blks) * subs + forward(sub, step, subs) for part in range(blks)]
        ).astype(jnp.int32)
        return products(
            sources, adjacency[0], target_block[0], source_block[0], slot_counts[0], ids
        )

    weights = [weight] + [fetch(weight, "feat", step) for step in range(1, feats)]
    arrived = [send(local(step), "sub", step) for step in range(1, subs)]
    chip = pair_sum(local(0), arrived)
    others = [send(chip[step], "blk", step) for step in range(1, blks)]
    ahead = jnp.stack([forward(feat, step, feats) for step in range(feats)]).astype(jnp.int32)
    behind = jnp.stack([backward(feat, step, feats) for step in range(feats)]).astype(jnp.int32)
    dealt = deal(ahead, chip[0], others)
    hidden = [dealt[0]] + [send(dealt[step], "feat", step) for step in range(1, feats)]
    outs = layer(behind, hidden, weights)
    done = [outs[0]] + [send(outs[step], "feat", step) for step in range(1, feats)]
    return gather_rows(behind, done)


def solution(mesh):
    return jax.shard_map(
        body,
        mesh=mesh,
        in_specs=(
            P(("blk", "sub"), "feat"),
            P(("blk", "sub"), None, None, None, None),
            P(("blk", "sub"), None, None),
            P(("blk", "sub"), None, None),
            P(("blk", "sub"), None),
            P(None, "feat"),
        ),
        out_specs=P(("blk", "sub"), "feat"),
        check_vma=False,
    )
```

```python
import functools

import jax
import jax.numpy as jnp
from jax import lax
from jax.experimental import pallas as pl
from jax.experimental.pallas import tpu as pltpu
from jax.sharding import PartitionSpec as P

TGT_DEV = 1024
GROUP = 8
PRODUCTS_VMEM = 54 * 2**20
SMALL_VMEM = 10 * 2**20


def forward(index, step, size):
    if size & (size - 1) == 0:
        return index ^ step
    return (index + step) % size


def backward(index, step, size):
    if size & (size - 1) == 0:
        return index ^ step
    return (index + size - step) % size


def send(value, axis, step):
    size = lax.axis_size(axis)
    return lax.ppermute(value, axis, [(i, forward(i, step, size)) for i in range(size)])


def fetch(value, axis, step):
    size = lax.axis_size(axis)
    return lax.ppermute(value, axis, [(forward(i, step, size), i) for i in range(size)])


def products_kernel(target, source, count, ids, src_hbm, adj_hbm, out, src, adj, acc, src_sem, adj_sem):
    step = pl.program_id(0)
    pieces, slots, block, _ = adj.shape
    targets = acc.shape[0] - 1
    src_copy = pltpu.make_async_copy(src_hbm, src, src_sem)

    def tiles(piece, group):
        rows = pl.ds(group * GROUP, GROUP)
        return pltpu.make_async_copy(
            adj_hbm.at[ids[piece], rows], adj.at[piece, rows], adj_sem.at[piece, group]
        )

    def groups(piece):
        return (count[ids[piece]] + GROUP - 1) // GROUP

    @pl.when(step == 0)
    def _():
        src_copy.start()

        @pl.loop(0, pieces)
        def _(piece):
            @pl.loop(0, groups(piece))
            def _(group):
                tiles(piece, group).start()

        src_copy.wait()

    here = ids[step]
    acc[...] = jnp.zeros_like(acc)

    @pl.loop(0, groups(step))
    def _(group):
        tiles(step, group).wait()
        for lane in range(GROUP):
            slot = group * GROUP + lane
            row = jnp.where(slot < count[here], target[here, slot], targets)
            rows = pl.ds(pl.multiple_of(source[here, slot] * block, block), block)
            acc[row] += jnp.dot(adj[step, slot], src[rows, :], preferred_element_type=jnp.float32)

    for row in range(targets):
        out[0, row * block : (row + 1) * block, :] = acc[row].astype(out.dtype)


def products(sources, adjacency, target, source, count, ids, dtype):
    _, slots, block, _ = adjacency.shape
    pieces = ids.shape[0]
    feat = sources.shape[1]
    return pl.pallas_call(
        products_kernel,
        grid_spec=pltpu.PrefetchScalarGridSpec(
            num_scalar_prefetch=4,
            grid=(pieces,),
            in_specs=[pl.BlockSpec(memory_space=pltpu.HBM)] * 2,
            out_specs=pl.BlockSpec((1, TGT_DEV, feat), lambda step, *_: (step, 0, 0)),
            scratch_shapes=[
                pltpu.VMEM(sources.shape, sources.dtype),
                pltpu.VMEM((pieces, slots, block, block), adjacency.dtype),
                pltpu.VMEM((TGT_DEV // block + 1, block, feat), jnp.float32),
                pltpu.SemaphoreType.DMA,
                pltpu.SemaphoreType.DMA((pieces, slots // GROUP)),
            ],
        ),
        out_shape=jax.ShapeDtypeStruct((pieces, TGT_DEV, feat), dtype),
        compiler_params=pltpu.CompilerParams(vmem_limit_bytes=PRODUCTS_VMEM),
        cost_estimate=pl.CostEstimate(
            flops=2 * pieces * slots * block * block * feat,
            bytes_accessed=2 * (sources.size + pieces * slots * block * block),
            transcendentals=0,
        ),
        name="products",
    )(target, source, count, ids, sources, adjacency)


def pair_sum_kernel(own, *refs):
    parts = own.shape[0]
    others, outs = refs[:-parts], refs[-parts:]
    for part in range(parts):
        total = own[part].astype(jnp.float32)
        for other in others:
            total += other[part].astype(jnp.float32)
        outs[part][...] = total.astype(outs[part].dtype)


def pair_sum(own, others):
    parts, rows, feat = own.shape
    vmem = pl.BlockSpec(memory_space=pltpu.VMEM)
    return pl.pallas_call(
        pair_sum_kernel,
        in_specs=[vmem] * (1 + len(others)),
        out_specs=[vmem] * parts,
        out_shape=[
            jax.ShapeDtypeStruct((rows, feat), jnp.float32 if part == 0 else jnp.bfloat16)
            for part in range(parts)
        ],
        compiler_params=pltpu.CompilerParams(vmem_limit_bytes=SMALL_VMEM),
        cost_estimate=pl.CostEstimate(
            flops=own.size * len(others), bytes_accessed=6 * own.size, transcendentals=0
        ),
        name="pair_sum",
    )(own, *others)


def deal_kernel(places, own, *refs):
    quarters = places.shape[0]
    others, outs = refs[:-quarters], refs[-quarters:]
    rows = outs[0].shape[0]
    for quarter in range(quarters):
        here = pl.ds(pl.multiple_of(places[quarter] * rows, rows), rows)
        total = own[here, :]
        for other in others:
            total += other[here, :].astype(jnp.float32)
        outs[quarter][...] = total.astype(jnp.bfloat16)


def deal(places, own, others):
    quarters = places.shape[0]
    rows, feat = own.shape
    vmem = pl.BlockSpec(memory_space=pltpu.VMEM)
    return pl.pallas_call(
        deal_kernel,
        in_specs=[pl.BlockSpec(memory_space=pltpu.SMEM)] + [vmem] * (1 + len(others)),
        out_specs=[vmem] * quarters,
        out_shape=[jax.ShapeDtypeStruct((rows // quarters, feat), jnp.bfloat16)] * quarters,
        compiler_params=pltpu.CompilerParams(vmem_limit_bytes=SMALL_VMEM),
        cost_estimate=pl.CostEstimate(
            flops=own.size * len(others), bytes_accessed=10 * own.size, transcendentals=0
        ),
        name="deal",
    )(places, own, *others)


def layer_kernel(shares, places, *refs):
    parts = places.shape[0] // 2
    count = 1 + (parts - 1) * shares
    hidden, weights = refs[:parts], refs[parts : parts + count]
    outs, held = refs[parts + count : -1], refs[-1]
    depth = held.shape[2]
    for part in range(parts):
        held[places[part]] = hidden[part][...]

    def multiply(first, ref):
        total = None
        for inner in range(ref.shape[0] // depth):
            rows = ref[inner * depth : (inner + 1) * depth, :]
            term = jnp.dot(held[first + inner], rows, preferred_element_type=jnp.float32)
            total = term if total is None else total + term
        return total

    for part in range(parts):
        if part == 0:
            total = multiply(0, weights[0])
        else:
            total = None
            for share in range(shares):
                ref = weights[1 + (part - 1) * shares + share]
                term = multiply(places[parts + share] * (parts // shares), ref)
                total = term if total is None else total + term
        outs[part][...] = jnp.maximum(total, 0.0).astype(outs[part].dtype)


def layer(places, hidden, weights, shares):
    parts = len(hidden)
    rows, feat = hidden[0].shape
    depth, columns = weights[0].shape
    vmem = pl.BlockSpec(memory_space=pltpu.VMEM)
    return pl.pallas_call(
        functools.partial(layer_kernel, shares),
        in_specs=[pl.BlockSpec(memory_space=pltpu.SMEM)] + [vmem] * (parts + len(weights)),
        out_specs=[vmem] * parts,
        out_shape=[jax.ShapeDtypeStruct((rows, columns), jnp.bfloat16)] * parts,
        scratch_shapes=[pltpu.VMEM((parts, rows, feat), jnp.bfloat16)],
        compiler_params=pltpu.CompilerParams(vmem_limit_bytes=SMALL_VMEM),
        cost_estimate=pl.CostEstimate(
            flops=2 * rows * depth * columns * parts,
            bytes_accessed=2 * parts * depth * columns,
            transcendentals=0,
        ),
        name="layer",
    )(places, *hidden, *weights)


def gather_rows_kernel(places, *refs):
    out = refs[-1]
    for part, piece in enumerate(refs[:-1]):
        rows = piece.shape[0]
        out[pl.ds(pl.multiple_of(places[part] * rows, rows), rows), :] = piece[...]


def gather_rows(places, pieces):
    rows, columns = pieces[0].shape
    vmem = pl.BlockSpec(memory_space=pltpu.VMEM)
    return pl.pallas_call(
        gather_rows_kernel,
        in_specs=[pl.BlockSpec(memory_space=pltpu.SMEM)] + [vmem] * len(pieces),
        out_specs=vmem,
        out_shape=jax.ShapeDtypeStruct((rows * len(pieces), columns), pieces[0].dtype),
        compiler_params=pltpu.CompilerParams(vmem_limit_bytes=SMALL_VMEM),
        name="gather_rows",
    )(places, *pieces)


def body(sources, adjacency, target_block, source_block, slot_counts, weight):
    blks, subs, feats = (lax.axis_size(axis) for axis in ("blk", "sub", "feat"))
    blk, sub, feat = (lax.axis_index(axis) for axis in ("blk", "sub", "feat"))

    def local(step, dtype):
        ids = jnp.stack(
            [forward(blk, part, blks) * subs + forward(sub, step, subs) for part in range(blks)]
        ).astype(jnp.int32)
        return products(
            sources, adjacency[0], target_block[0], source_block[0], slot_counts[0], ids, dtype
        )

    def exchange(parts, axis):
        size = lax.axis_size(axis)
        got = {step: send(parts[step], axis, step) for step in reversed(range(1, size))}
        return [got[step] for step in range(1, size)]

    share_rows = weight.shape[0] // subs
    share = lax.dynamic_slice_in_dim(weight, sub * share_rows, share_rows, 0)

    arrived = [send(local(step, jnp.bfloat16), "sub", step) for step in range(1, subs)]
    chip = pair_sum(local(0, jnp.float32), arrived)
    *chip, share = lax.optimization_barrier((*chip, share))
    others = exchange(chip, "blk")
    shares = [fetch(share, "feat", step) for step in range(1, feats)]
    ahead = jnp.stack([forward(feat, step, feats) for step in range(feats)]).astype(jnp.int32)
    behind = jnp.stack([backward(feat, step, feats) for step in range(feats)]).astype(jnp.int32)
    turns = jnp.stack([forward(sub, step, subs) for step in range(subs)]).astype(jnp.int32)
    dealt = deal(ahead, chip[0], others)
    hidden = [dealt[0]] + exchange(dealt, "feat")
    weights = [weight]
    for part in shares:
        weights += [part] + [fetch(part, "sub", step) for step in range(1, subs)]
    outs = layer(jnp.concatenate([behind, behind * 0 + jnp.resize(turns, feats)]), hidden, weights, subs)
    done = [outs[0]] + exchange(outs, "feat")
    return gather_rows(behind, done)


def solution(mesh):
    return jax.shard_map(
        body,
        mesh=mesh,
        in_specs=(
            P(("blk", "sub"), "feat"),
            P(("blk", "sub"), None, None, None, None),
            P(("blk", "sub"), None, None),
            P(("blk", "sub"), None, None),
            P(("blk", "sub"), None),
            P(None, "feat"),
        ),
        out_specs=P(("blk", "sub"), "feat"),
        check_vma=False,
    )
```

```python
import functools

import jax
import jax.numpy as jnp
from jax import lax
from jax.experimental import pallas as pl
from jax.experimental.pallas import tpu as pltpu
from jax.sharding import PartitionSpec as P

TGT_DEV = 1024
GROUP = 8
PAIRS = 8
PLAN_VMEM = 45 * 2**20
PRODUCTS_VMEM = 36 * 2**20
SMALL_VMEM = 10 * 2**20


def forward(index, step, size):
    if size & (size - 1) == 0:
        return index ^ step
    return (index + step) % size


def backward(index, step, size):
    if size & (size - 1) == 0:
        return index ^ step
    return (index + size - step) % size


def send(value, axis, step):
    size = lax.axis_size(axis)
    return lax.ppermute(value, axis, [(i, forward(i, step, size)) for i in range(size)])


def fetch(value, axis, step):
    size = lax.axis_size(axis)
    return lax.ppermute(value, axis, [(forward(i, step, size), i) for i in range(size)])


def plan_sizes(slots, targets, blocks):
    rows = -(-((slots + targets) // 2) // PAIRS) * PAIRS
    return rows, slots.bit_length(), (targets - 1).bit_length(), (blocks - 1).bit_length()


class Tiles:
    def __init__(self, adj, tiles, sem, numbers, counts):
        self.adj, self.tiles, self.sem = adj, tiles, sem
        self.numbers, self.counts = numbers, counts

    def copy(self, part, group):
        some = pl.ds(group * GROUP, GROUP)
        return pltpu.make_async_copy(
            self.adj.at[0, self.numbers[part], some],
            self.tiles.at[part, some],
            self.sem.at[part, group],
        )

    def each(self, act):
        for part, count in enumerate(self.counts):

            @pl.loop(0, (count + GROUP - 1) // GROUP)
            def _(group):
                act(self.copy(part, group))

    def start(self):
        self.each(lambda copy: copy.start())
        for part in range(len(self.counts)):
            zero = jnp.zeros(self.tiles.shape[2:], self.tiles.dtype)
            self.tiles[part, self.tiles.shape[1] - 1] = zero

    def wait(self):
        self.each(lambda copy: copy.wait())


def tiles_shape(adjacency, pieces):
    slots, block = adjacency.shape[2:4]
    return jax.ShapeDtypeStruct((pieces, slots + 1, block, block), adjacency.dtype)


def tiles_sems(adjacency, pieces):
    return pltpu.SemaphoreType.DMA((pieces, adjacency.shape[2] // GROUP))


def plan_kernel(
    targets, blocks, later, ids, count, target_hbm, source_hbm, src_hbm, adj_hbm, weight,
    out, src, tiles, share, target_ref, source_ref, sems, tile_sems,
):
    small = [
        pltpu.make_async_copy(target_hbm, target_ref, sems.at[0]),
        pltpu.make_async_copy(source_hbm, source_ref, sems.at[1]),
    ]
    large = pltpu.make_async_copy(src_hbm, src, sems.at[2])
    height = share.shape[0]
    mine = pl.ds(pl.multiple_of(ids[ids.shape[0] - 1] * height, height), height)
    part_copy = pltpu.make_async_copy(weight.at[mine], share, sems.at[3])
    part_copy.start()
    for copy in small:
        copy.start()
    large.start()
    numbers = [ids[place] for place in later]
    loads = Tiles(adj_hbm, tiles, tile_sems, numbers, [count[0, number] for number in numbers])
    loads.start()
    for copy in small:
        copy.wait()
    pieces, slots = target_ref.shape[1:]
    rows, slot_bits, target_bits, block_bits = plan_sizes(slots, targets, blocks)

    def iota(shape, axis):
        return lax.broadcasted_iota(jnp.int32, shape, axis)

    def exact(left, right):
        return jnp.dot(
            left.astype(jnp.bfloat16), right.astype(jnp.bfloat16), preferred_element_type=jnp.float32
        )

    lane = iota((1, slots), 1)
    hot, rest = [], []
    for part in range(pieces):
        piece = ids[part]
        live = lane < count[0, piece]
        target = target_ref[0, pl.ds(piece, 1), :]
        rest.append((live, target, source_ref[0, pl.ds(piece, 1), :]))
        hot.append(((iota((targets, slots), 0) == target) & live).astype(jnp.float32))
    every = jnp.concatenate(hot, axis=0)
    before = (iota((slots, slots), 0) < iota((slots, slots), 1)).astype(jnp.float32)
    order = exact(every, before).astype(jnp.int32)
    pairs = (jnp.sum(every, axis=1, keepdims=True).astype(jnp.int32) + 1) // 2
    size = pieces * targets
    above = (iota((size, size), 1) < iota((size, size), 0)) & (
        iota((size, size), 1) // targets == iota((size, size), 0) // targets
    )
    wide = jnp.broadcast_to(pairs.astype(jnp.float32), (size, slots))
    first = exact(above.astype(jnp.float32), wide).astype(jnp.int32)
    place = every * (first + order // 2).astype(jnp.float32)
    odd = every * (order % 2).astype(jnp.float32)

    column = iota((rows, pieces), 1)
    plan = jnp.zeros((rows, pieces), jnp.int32)
    extra = jnp.zeros((8, pieces), jnp.int32)
    small = iota((8, pieces), 0)
    for part in range(pieces):
        live, target, source = rest[part]
        mine = slice(part * targets, (part + 1) * targets)
        index = jnp.sum(place[mine], axis=0, keepdims=True).astype(jnp.int32)
        second = jnp.sum(odd[mine], axis=0, keepdims=True) > 0
        hit = (iota((rows, slots), 0) == index) & live
        code = (slots - lane) | (source << slot_bits)
        one = code | (target << (slot_bits + block_bits))
        one = jnp.where(hit & jnp.logical_not(second), one.astype(jnp.float32), 0.0)
        two = jnp.where(hit & second, code.astype(jnp.float32), 0.0)
        one = jnp.sum(one, axis=1, keepdims=True).astype(jnp.int32)
        two = jnp.sum(two, axis=1, keepdims=True).astype(jnp.int32)
        both = one | (two << (slot_bits + block_bits + target_bits))
        plan = jnp.where(column == part, both, plan)
        total = jnp.sum(pairs[mine].astype(jnp.float32), axis=0, keepdims=True).astype(jnp.int32)
        values = jnp.where(small == 0, total, jnp.where(small == 1, count[0, ids[part]], ids[part]))
        extra = jnp.where(iota((8, pieces), 1) == part, values, extra)
    out[0:rows, :] = plan
    out[rows:, :] = extra
    large.wait()
    loads.wait()
    part_copy.wait()


def make_plan(target_block, source_block, slot_counts, ids, sources, adjacency, weight, subs, later):
    _, pieces, slots = target_block.shape
    block = adjacency.shape[-1]
    targets, blocks = TGT_DEV // block, sources.shape[0] // block
    rows = plan_sizes(slots, targets, blocks)[0]
    smem, vmem, hbm = (
        pl.BlockSpec(memory_space=space) for space in (pltpu.SMEM, pltpu.VMEM, pltpu.HBM)
    )
    return pl.pallas_call(
        functools.partial(plan_kernel, targets, blocks, later),
        in_specs=[smem, smem] + [hbm] * 5,
        out_specs=[vmem] * 4,
        out_shape=[
            jax.ShapeDtypeStruct((rows + 8, pieces), jnp.int32),
            jax.ShapeDtypeStruct(sources.shape, sources.dtype),
            tiles_shape(adjacency, len(later)),
            jax.ShapeDtypeStruct((weight.shape[0] // subs, weight.shape[1]), weight.dtype),
        ],
        scratch_shapes=[
            pltpu.VMEM(target_block.shape, target_block.dtype),
            pltpu.VMEM(source_block.shape, source_block.dtype),
            pltpu.SemaphoreType.DMA((4,)),
            tiles_sems(adjacency, len(later)),
        ],
        compiler_params=pltpu.CompilerParams(vmem_limit_bytes=PLAN_VMEM),
        name="plan",
    )(ids, slot_counts, target_block, source_block, sources, adjacency, weight)


def products_kernel(places, later, targets, plan, src, adj, *refs):
    slots, block = adj.shape[1] - 1, adj.shape[2]
    rows, slot_bits, target_bits, block_bits = plan_sizes(slots, targets, src.shape[0] // block)
    if later:
        adj_hbm, *outs, tiles, acc, sems = refs
        numbers = [plan[rows + 2, place] for place in later]
        counts = [plan[rows + 1, place] for place in later]
        loads = Tiles(adj_hbm, tiles, sems, numbers, counts)
        loads.start()
    else:
        *outs, acc = refs

    def field(code, start, width):
        return (code >> start) & ((1 << width) - 1)

    def source(number):
        return src[pl.ds(pl.multiple_of(number * block, block), block), :]

    for part, out in enumerate(outs):
        total = out if out.dtype == jnp.float32 else acc
        total[...] = jnp.zeros_like(total)

        @pl.loop(0, (plan[rows, places[part]] + PAIRS - 1) // PAIRS)
        def _(step):
            for lane in range(PAIRS):
                code = plan[step * PAIRS + lane, places[part]]
                half = code >> (slot_bits + block_bits + target_bits)
                one, two = (adj[part, slots - field(c, 0, slot_bits)] for c in (code, half))
                left = jnp.concatenate([one, two], axis=1)
                one, two = (source(field(c, slot_bits, block_bits)) for c in (code, half))
                right = jnp.concatenate([one, two], axis=0)
                start = field(code, slot_bits + block_bits, target_bits) * block
                at = pl.ds(pl.multiple_of(start, block), block)
                total[at, :] += jnp.dot(left, right, preferred_element_type=jnp.float32)

        if total is acc:
            out[...] = acc[...].astype(out.dtype)
    if later:
        loads.wait()


def products(sources, adjacency, tiles, plan, places, later, own):
    block = adjacency.shape[3]
    pieces = len(places)
    feat = sources.shape[1]
    smem, vmem, hbm = (
        pl.BlockSpec(memory_space=space) for space in (pltpu.SMEM, pltpu.VMEM, pltpu.HBM)
    )
    outs = [
        jax.ShapeDtypeStruct((TGT_DEV, feat), jnp.float32 if place < own else jnp.bfloat16)
        for place in places
    ]
    scratch = [pltpu.VMEM((TGT_DEV, feat), jnp.float32)]
    if later:
        outs.append(tiles_shape(adjacency, len(later)))
        scratch.append(tiles_sems(adjacency, len(later)))
    got = pl.pallas_call(
        functools.partial(products_kernel, places, later, TGT_DEV // block),
        in_specs=[smem, vmem, vmem] + ([hbm] if later else []),
        out_specs=[vmem] * len(outs),
        out_shape=outs,
        scratch_shapes=scratch,
        compiler_params=pltpu.CompilerParams(vmem_limit_bytes=PRODUCTS_VMEM),
        cost_estimate=pl.CostEstimate(flops=2**20, bytes_accessed=1024, transcendentals=0),
        name="products",
    )(plan, sources, tiles, *([adjacency] if later else []))
    return list(got[:pieces]), (got[pieces] if later else None)


def pair_sum_kernel(*refs):
    parts = len(refs) // 3
    for own, other, out in zip(refs[:parts], refs[parts : 2 * parts], refs[2 * parts :]):
        out[...] = (own[...] + other[...].astype(jnp.float32)).astype(out.dtype)


def pair_sum(own, others):
    vmem = pl.BlockSpec(memory_space=pltpu.VMEM)
    return pl.pallas_call(
        pair_sum_kernel,
        in_specs=[vmem] * (2 * len(own)),
        out_specs=[vmem] * len(own),
        out_shape=[jax.ShapeDtypeStruct(part.shape, jnp.bfloat16) for part in own],
        compiler_params=pltpu.CompilerParams(vmem_limit_bytes=SMALL_VMEM),
        cost_estimate=pl.CostEstimate(
            flops=own[0].size * len(own), bytes_accessed=6 * own[0].size * len(own), transcendentals=0
        ),
        name="pair_sum",
    )(*own, *others)


def deal_kernel(quarters, first, places, own, *refs):
    others, outs = refs[:-quarters], refs[-quarters:]
    rows = outs[0].shape[0]
    for quarter in range(quarters):
        here = pl.ds(pl.multiple_of(places[first + quarter] * rows, rows), rows)
        total = own[here, :]
        for other in others:
            total += other[here, :].astype(jnp.float32)
        outs[quarter][...] = total.astype(jnp.bfloat16)


def deal(quarters, first, places, own, others):
    rows, feat = own.shape
    vmem = pl.BlockSpec(memory_space=pltpu.VMEM)
    return pl.pallas_call(
        functools.partial(deal_kernel, quarters, first),
        in_specs=[pl.BlockSpec(memory_space=pltpu.SMEM)] + [vmem] * (1 + len(others)),
        out_specs=[vmem] * quarters,
        out_shape=[jax.ShapeDtypeStruct((rows // quarters, feat), jnp.bfloat16)] * quarters,
        compiler_params=pltpu.CompilerParams(vmem_limit_bytes=SMALL_VMEM),
        cost_estimate=pl.CostEstimate(
            flops=own.size * len(others), bytes_accessed=10 * own.size, transcendentals=0
        ),
        name="deal",
    )(places, own, *others)


def layer_kernel(parts, first, places, *refs):
    half = places[first + parts]
    hidden, weights, outs = refs[:parts], refs[parts:-parts - 1], refs[-parts - 1 : -1]
    held = refs[-1]
    depth = hidden[0].shape[1]
    middle = held.shape[1] // 2
    for part, ref in enumerate(hidden):
        at = pl.multiple_of(places[first + part] * depth, depth)
        held[:, pl.ds(at, depth)] = ref[...]
    for part, out in enumerate(outs):
        if part == 0:
            total = jnp.dot(held[...], weights[0][...], preferred_element_type=jnp.float32)
        else:
            total = 0.0
            for side in range(2):
                at = pl.multiple_of((half ^ side) * middle, middle)
                share = weights[2 * part - 1 + side]
                total += jnp.dot(
                    held[:, pl.ds(at, middle)], share[...], preferred_element_type=jnp.float32
                )
        out[...] = jnp.maximum(total, 0.0).astype(out.dtype)


def layer(first, places, hidden, weights):
    parts = len(hidden)
    rows, feat = hidden[0].shape
    depth, columns = weights[0].shape
    vmem = pl.BlockSpec(memory_space=pltpu.VMEM)
    return pl.pallas_call(
        functools.partial(layer_kernel, parts, first),
        in_specs=[pl.BlockSpec(memory_space=pltpu.SMEM)] + [vmem] * (parts + len(weights)),
        out_specs=[vmem] * parts,
        out_shape=[jax.ShapeDtypeStruct((rows, columns), jnp.bfloat16)] * parts,
        scratch_shapes=[pltpu.VMEM((rows, parts * feat), jnp.bfloat16)],
        compiler_params=pltpu.CompilerParams(vmem_limit_bytes=SMALL_VMEM),
        cost_estimate=pl.CostEstimate(
            flops=2 * rows * depth * columns * parts,
            bytes_accessed=2 * parts * depth * columns,
            transcendentals=0,
        ),
        name="layer",
    )(places, *hidden, *weights)


def gather_rows_kernel(first, places, *refs):
    out = refs[-1]
    for part, piece in enumerate(refs[:-1]):
        rows = piece.shape[0]
        out[pl.ds(pl.multiple_of(places[first + part] * rows, rows), rows), :] = piece[...]


def gather_rows(first, places, pieces):
    rows, columns = pieces[0].shape
    vmem = pl.BlockSpec(memory_space=pltpu.VMEM)
    return pl.pallas_call(
        functools.partial(gather_rows_kernel, first),
        in_specs=[pl.BlockSpec(memory_space=pltpu.SMEM)] + [vmem] * len(pieces),
        out_specs=vmem,
        out_shape=jax.ShapeDtypeStruct((rows * len(pieces), columns), pieces[0].dtype),
        compiler_params=pltpu.CompilerParams(vmem_limit_bytes=SMALL_VMEM),
        name="gather_rows",
    )(places, *pieces)


def body(sources, adjacency, target_block, source_block, slot_counts, weight):
    blks, subs, feats = (lax.axis_size(axis) for axis in ("blk", "sub", "feat"))
    blk, sub, feat = (lax.axis_index(axis) for axis in ("blk", "sub", "feat"))
    pieces = [
        forward(blk, part, blks) * subs + forward(sub, step, subs)
        for step in range(subs)
        for part in range(blks)
    ]
    ahead = [forward(feat, step, feats) for step in range(feats)]
    behind = [backward(feat, step, feats) for step in range(feats)]
    places = jnp.stack(pieces + ahead + behind + [sub]).astype(jnp.int32)
    at_ahead, at_behind = len(pieces), len(pieces) + feats

    def exchange(parts, axis):
        size = lax.axis_size(axis)
        got = {step: send(parts[step], axis, step) for step in reversed(range(1, size))}
        return [got[step] for step in range(1, size)]

    far, near = [blks - 1], list(range(blks - 2, 0, -1))
    other = [blks + part for part in range(blks)]
    calls = [
        [other[part] for part in far], far, [other[part] for part in near], near + [other[0]], [0], []
    ]
    plan, held, tiles, share = make_plan(
        target_block, source_block, slot_counts, places, sources, adjacency, weight, subs, calls[0]
    )
    shares = {step: fetch(share, "feat", step) for step in reversed(range(1, feats))}

    def local(number, after):
        nonlocal tiles
        turn, now, *_ = lax.optimization_barrier((plan, tiles, *after))
        made, tiles = products(held, adjacency, now, turn, calls[number], calls[number + 1], blks)
        return made

    others = {}
    away = local(0, [])
    arrived = [send(value, "sub", 1) for value in away]
    kept = local(1, away)
    sums = list(pair_sum(kept, arrived))
    others.update((part, send(value, "blk", part)) for part, value in zip(far, sums))
    away = local(2, sums)
    arrived = [send(value, "sub", 1) for value in away]
    *kept, last = local(3, away)
    sums = list(pair_sum(kept, arrived))
    others.update((part, send(value, "blk", part)) for part, value in zip(near, sums))
    (kept,) = local(4, sums)
    kept, shares = lax.optimization_barrier((kept, shares))
    dealt = deal(feats, at_ahead, places, kept, [send(last, "sub", 1)] + [others[part] for part in range(1, blks)])
    *dealt, shares = lax.optimization_barrier((*dealt, shares))
    hidden = [dealt[0]] + exchange(dealt, "feat")
    weights = [weight]
    for step in range(1, feats):
        weights += [shares[step], send(shares[step], "sub", 1)]
    outs = layer(at_behind, places, hidden, weights)
    done = [outs[0]] + exchange(outs, "feat")
    return gather_rows(at_behind, places, done)


def solution(mesh):
    return jax.shard_map(
        body,
        mesh=mesh,
        in_specs=(
            P(("blk", "sub"), "feat"),
            P(("blk", "sub"), None, None, None, None),
            P(("blk", "sub"), None, None),
            P(("blk", "sub"), None, None),
            P(("blk", "sub"), None),
            P(None, "feat"),
        ),
        out_specs=P(("blk", "sub"), "feat"),
        check_vma=False,
    )
```

```python
import functools

import jax
import jax.numpy as jnp
from jax import lax
from jax.experimental import pallas as pl
from jax.experimental.pallas import tpu as pltpu
from jax.sharding import PartitionSpec as P

TGT_DEV = 1024
GROUP = 8
PAIRS = 8
PLAN_VMEM = 45 * 2**20
PRODUCTS_VMEM = 36 * 2**20
SMALL_VMEM = 10 * 2**20


def forward(index, step, size):
    if size & (size - 1) == 0:
        return index ^ step
    return (index + step) % size


def backward(index, step, size):
    if size & (size - 1) == 0:
        return index ^ step
    return (index + size - step) % size


def send(value, axis, step):
    size = lax.axis_size(axis)
    return lax.ppermute(value, axis, [(i, forward(i, step, size)) for i in range(size)])


def fetch(value, axis, step):
    size = lax.axis_size(axis)
    return lax.ppermute(value, axis, [(forward(i, step, size), i) for i in range(size)])


def plan_sizes(slots, targets, blocks):
    rows = -(-((slots + targets) // 2) // PAIRS) * PAIRS
    return rows, slots.bit_length(), (targets - 1).bit_length(), (blocks - 1).bit_length()


class Tiles:
    def __init__(self, adj, tiles, sem, numbers, counts):
        self.adj, self.tiles, self.sem = adj, tiles, sem
        self.numbers, self.counts = numbers, counts

    def copy(self, part, group):
        some = pl.ds(group * GROUP, GROUP)
        return pltpu.make_async_copy(
            self.adj.at[0, self.numbers[part], some],
            self.tiles.at[part, some],
            self.sem.at[part, group],
        )

    def each(self, act):
        for part, count in enumerate(self.counts):

            @pl.loop(0, (count + GROUP - 1) // GROUP)
            def _(group):
                act(self.copy(part, group))

    def start(self):
        self.each(lambda copy: copy.start())
        for part in range(len(self.counts)):
            zero = jnp.zeros(self.tiles.shape[2:], self.tiles.dtype)
            self.tiles[part, self.tiles.shape[1] - 1] = zero

    def wait(self):
        self.each(lambda copy: copy.wait())


def tiles_shape(adjacency, pieces):
    slots, block = adjacency.shape[2:4]
    return jax.ShapeDtypeStruct((pieces, slots + 1, block, block), adjacency.dtype)


def tiles_sems(adjacency, pieces):
    return pltpu.SemaphoreType.DMA((pieces, adjacency.shape[2] // GROUP))


def plan_kernel(
    targets, blocks, later, ids, count, slots_ref, src_hbm, adj_hbm, out, src, tiles, sem, tile_sems
):
    large = pltpu.make_async_copy(src_hbm, src, sem)
    large.start()
    numbers = [ids[place] for place in later]
    loads = Tiles(adj_hbm, tiles, tile_sems, numbers, [count[0, number] for number in numbers])
    loads.start()
    pieces, slots = slots_ref.shape
    rows, slot_bits, target_bits, block_bits = plan_sizes(slots, targets, blocks)

    def iota(shape, axis):
        return lax.broadcasted_iota(jnp.int32, shape, axis)

    def exact(left, right):
        return jnp.dot(
            left.astype(jnp.bfloat16), right.astype(jnp.bfloat16), preferred_element_type=jnp.float32
        )

    lane = iota((1, slots), 1)
    hot, rest = [], []
    for part in range(pieces):
        piece = ids[part]
        live = lane < count[0, piece]
        both = slots_ref[pl.ds(piece, 1), :]
        target = both >> block_bits
        rest.append((live, target, both & ((1 << block_bits) - 1)))
        hot.append(((iota((targets, slots), 0) == target) & live).astype(jnp.float32))
    every = jnp.concatenate(hot, axis=0)
    before = (iota((slots, slots), 0) < iota((slots, slots), 1)).astype(jnp.float32)
    order = exact(every, before).astype(jnp.int32)
    pairs = (jnp.sum(every, axis=1, keepdims=True).astype(jnp.int32) + 1) // 2
    size = pieces * targets
    above = (iota((size, size), 1) < iota((size, size), 0)) & (
        iota((size, size), 1) // targets == iota((size, size), 0) // targets
    )
    wide = jnp.broadcast_to(pairs.astype(jnp.float32), (size, slots))
    first = exact(above.astype(jnp.float32), wide).astype(jnp.int32)
    place = every * (first + order // 2).astype(jnp.float32)
    odd = every * (order % 2).astype(jnp.float32)

    column = iota((rows, pieces), 1)
    plan = jnp.zeros((rows, pieces), jnp.int32)
    extra = jnp.zeros((8, pieces), jnp.int32)
    small = iota((8, pieces), 0)
    for part in range(pieces):
        live, target, source = rest[part]
        mine = slice(part * targets, (part + 1) * targets)
        index = jnp.sum(place[mine], axis=0, keepdims=True).astype(jnp.int32)
        second = jnp.sum(odd[mine], axis=0, keepdims=True) > 0
        hit = (iota((rows, slots), 0) == index) & live
        code = (slots - lane) | (source << slot_bits)
        one = code | (target << (slot_bits + block_bits))
        one = jnp.where(hit & jnp.logical_not(second), one.astype(jnp.float32), 0.0)
        two = jnp.where(hit & second, code.astype(jnp.float32), 0.0)
        one = jnp.sum(one, axis=1, keepdims=True).astype(jnp.int32)
        two = jnp.sum(two, axis=1, keepdims=True).astype(jnp.int32)
        both = one | (two << (slot_bits + block_bits + target_bits))
        plan = jnp.where(column == part, both, plan)
        total = jnp.sum(pairs[mine].astype(jnp.float32), axis=0, keepdims=True).astype(jnp.int32)
        values = jnp.where(small == 0, total, jnp.where(small == 1, count[0, ids[part]], ids[part]))
        extra = jnp.where(iota((8, pieces), 1) == part, values, extra)
    out[0:rows, :] = plan
    out[rows:, :] = extra
    large.wait()
    loads.wait()


def make_plan(target_block, source_block, slot_counts, places, sources, adjacency, later):
    _, pieces, slots = target_block.shape
    block = adjacency.shape[-1]
    targets, blocks = TGT_DEV // block, sources.shape[0] // block
    rows, _, _, block_bits = plan_sizes(slots, targets, blocks)
    smem, vmem, hbm = (
        pl.BlockSpec(memory_space=space) for space in (pltpu.SMEM, pltpu.VMEM, pltpu.HBM)
    )
    return pl.pallas_call(
        functools.partial(plan_kernel, targets, blocks, later),
        in_specs=[smem, smem, vmem, hbm, hbm],
        out_specs=[vmem] * 3,
        out_shape=[
            jax.ShapeDtypeStruct((rows + 8, pieces), jnp.int32),
            jax.ShapeDtypeStruct(sources.shape, sources.dtype),
            tiles_shape(adjacency, len(later)),
        ],
        scratch_shapes=[pltpu.SemaphoreType.DMA, tiles_sems(adjacency, len(later))],
        compiler_params=pltpu.CompilerParams(vmem_limit_bytes=PLAN_VMEM),
        name="plan",
    )(places, slot_counts, (target_block[0] << block_bits) + source_block[0], sources, adjacency)


def products_kernel(places, later, targets, shared, plan, src, adj, *refs):
    slots, block = adj.shape[1] - 1, adj.shape[2]
    rows, slot_bits, target_bits, block_bits = plan_sizes(slots, targets, src.shape[0] // block)
    refs = list(refs)
    if shared:
        whole, weight = refs.pop(0), refs.pop(0)
        sem, share = refs.pop(), refs.pop(-shared)
        height = share.shape[0]
        mine = pl.ds(pl.multiple_of(whole[whole.shape[0] - 1] * height, height), height)
        taking = pltpu.make_async_copy(weight.at[mine], share, sem)
        taking.start()
    if later:
        adj_hbm, *outs, tiles, acc, sems = refs
        numbers = [plan[rows + 2, place] for place in later]
        counts = [plan[rows + 1, place] for place in later]
        loads = Tiles(adj_hbm, tiles, sems, numbers, counts)
        loads.start()
    else:
        *outs, acc = refs

    def field(code, start, width):
        return (code >> start) & ((1 << width) - 1)

    def source(number):
        return src[pl.ds(pl.multiple_of(number * block, block), block), :]

    for part, out in enumerate(outs):
        total = out if out.dtype == jnp.float32 else acc
        total[...] = jnp.zeros_like(total)

        @pl.loop(0, (plan[rows, places[part]] + PAIRS - 1) // PAIRS)
        def _(step):
            for lane in range(PAIRS):
                code = plan[step * PAIRS + lane, places[part]]
                half = code >> (slot_bits + block_bits + target_bits)
                one, two = (adj[part, slots - field(c, 0, slot_bits)] for c in (code, half))
                left = jnp.concatenate([one, two], axis=1)
                one, two = (source(field(c, slot_bits, block_bits)) for c in (code, half))
                right = jnp.concatenate([one, two], axis=0)
                start = field(code, slot_bits + block_bits, target_bits) * block
                at = pl.ds(pl.multiple_of(start, block), block)
                total[at, :] += jnp.dot(left, right, preferred_element_type=jnp.float32)

        if total is acc:
            out[...] = acc[...].astype(out.dtype)
    if later:
        loads.wait()
    if shared:
        taking.wait()


def products(sources, adjacency, tiles, plan, places, later, own, taken=()):
    block = adjacency.shape[3]
    pieces = len(places)
    feat = sources.shape[1]
    smem, vmem, hbm = (
        pl.BlockSpec(memory_space=space) for space in (pltpu.SMEM, pltpu.VMEM, pltpu.HBM)
    )
    outs = [
        jax.ShapeDtypeStruct((TGT_DEV, feat), jnp.float32 if place < own else jnp.bfloat16)
        for place in places
    ]
    scratch = [pltpu.VMEM((TGT_DEV, feat), jnp.float32)]
    if later:
        outs.append(tiles_shape(adjacency, len(later)))
        scratch.append(tiles_sems(adjacency, len(later)))
    if taken:
        outs.append(jax.ShapeDtypeStruct((taken[2], taken[1].shape[1]), taken[1].dtype))
        scratch.append(pltpu.SemaphoreType.DMA)
    shared = len(scratch) if taken else 0
    got = pl.pallas_call(
        functools.partial(products_kernel, places, later, TGT_DEV // block, shared),
        in_specs=[smem, vmem, vmem] + ([smem, hbm] if taken else []) + ([hbm] if later else []),
        out_specs=[vmem] * len(outs),
        out_shape=outs,
        scratch_shapes=scratch,
        compiler_params=pltpu.CompilerParams(vmem_limit_bytes=PRODUCTS_VMEM),
        cost_estimate=pl.CostEstimate(flops=2**20, bytes_accessed=1024, transcendentals=0),
        name="products",
    )(plan, sources, tiles, *taken[:2], *([adjacency] if later else []))
    return list(got[:pieces]), (got[pieces] if later else None), got[-1]


def pair_sum_kernel(*refs):
    parts = len(refs) // 3
    for own, other, out in zip(refs[:parts], refs[parts : 2 * parts], refs[2 * parts :]):
        out[...] = (own[...] + other[...].astype(jnp.float32)).astype(out.dtype)


def pair_sum(own, others):
    vmem = pl.BlockSpec(memory_space=pltpu.VMEM)
    return pl.pallas_call(
        pair_sum_kernel,
        in_specs=[vmem] * (2 * len(own)),
        out_specs=[vmem] * len(own),
        out_shape=[jax.ShapeDtypeStruct(part.shape, jnp.bfloat16) for part in own],
        compiler_params=pltpu.CompilerParams(vmem_limit_bytes=SMALL_VMEM),
        cost_estimate=pl.CostEstimate(
            flops=own[0].size * len(own), bytes_accessed=6 * own[0].size * len(own), transcendentals=0
        ),
        name="pair_sum",
    )(*own, *others)


def deal_kernel(quarters, first, places, own, *refs):
    others, outs = refs[:-quarters], refs[-quarters:]
    rows = outs[0].shape[0]
    for quarter in range(quarters):
        here = pl.ds(pl.multiple_of(places[first + quarter] * rows, rows), rows)
        total = own[here, :]
        for other in others:
            total += other[here, :].astype(jnp.float32)
        outs[quarter][...] = total.astype(jnp.bfloat16)


def deal(quarters, first, places, own, others):
    rows, feat = own.shape
    vmem = pl.BlockSpec(memory_space=pltpu.VMEM)
    return pl.pallas_call(
        functools.partial(deal_kernel, quarters, first),
        in_specs=[pl.BlockSpec(memory_space=pltpu.SMEM)] + [vmem] * (1 + len(others)),
        out_specs=[vmem] * quarters,
        out_shape=[jax.ShapeDtypeStruct((rows // quarters, feat), jnp.bfloat16)] * quarters,
        compiler_params=pltpu.CompilerParams(vmem_limit_bytes=SMALL_VMEM),
        cost_estimate=pl.CostEstimate(
            flops=own.size * len(others), bytes_accessed=10 * own.size, transcendentals=0
        ),
        name="deal",
    )(places, own, *others)


def layer_kernel(parts, first, places, *refs):
    half = places[first + parts]
    hidden, weights, outs = refs[:parts], refs[parts:-parts - 1], refs[-parts - 1 : -1]
    held = refs[-1]
    depth = hidden[0].shape[1]
    middle = held.shape[1] // 2
    for part, ref in enumerate(hidden):
        at = pl.multiple_of(places[first + part] * depth, depth)
        held[:, pl.ds(at, depth)] = ref[...]
    for part, out in enumerate(outs):
        if part == 0:
            total = jnp.dot(held[...], weights[0][...], preferred_element_type=jnp.float32)
        else:
            total = 0.0
            for side in range(2):
                at = pl.multiple_of((half ^ side) * middle, middle)
                share = weights[2 * part - 1 + side]
                total += jnp.dot(
                    held[:, pl.ds(at, middle)], share[...], preferred_element_type=jnp.float32
                )
        out[...] = jnp.maximum(total, 0.0).astype(out.dtype)


def layer(first, places, hidden, weights):
    parts = len(hidden)
    rows, feat = hidden[0].shape
    depth, columns = weights[0].shape
    vmem = pl.BlockSpec(memory_space=pltpu.VMEM)
    return pl.pallas_call(
        functools.partial(layer_kernel, parts, first),
        in_specs=[pl.BlockSpec(memory_space=pltpu.SMEM)] + [vmem] * (parts + len(weights)),
        out_specs=[vmem] * parts,
        out_shape=[jax.ShapeDtypeStruct((rows, columns), jnp.bfloat16)] * parts,
        scratch_shapes=[pltpu.VMEM((rows, parts * feat), jnp.bfloat16)],
        compiler_params=pltpu.CompilerParams(vmem_limit_bytes=SMALL_VMEM),
        cost_estimate=pl.CostEstimate(
            flops=2 * rows * depth * columns * parts,
            bytes_accessed=2 * parts * depth * columns,
            transcendentals=0,
        ),
        name="layer",
    )(places, *hidden, *weights)


def gather_rows_kernel(first, places, *refs):
    out = refs[-1]
    for part, piece in enumerate(refs[:-1]):
        rows = piece.shape[0]
        out[pl.ds(pl.multiple_of(places[first + part] * rows, rows), rows), :] = piece[...]


def gather_rows(first, places, pieces):
    rows, columns = pieces[0].shape
    vmem = pl.BlockSpec(memory_space=pltpu.VMEM)
    return pl.pallas_call(
        functools.partial(gather_rows_kernel, first),
        in_specs=[pl.BlockSpec(memory_space=pltpu.SMEM)] + [vmem] * len(pieces),
        out_specs=vmem,
        out_shape=jax.ShapeDtypeStruct((rows * len(pieces), columns), pieces[0].dtype),
        compiler_params=pltpu.CompilerParams(vmem_limit_bytes=SMALL_VMEM),
        name="gather_rows",
    )(places, *pieces)


def body(sources, adjacency, target_block, source_block, slot_counts, weight):
    blks, subs, feats = (lax.axis_size(axis) for axis in ("blk", "sub", "feat"))
    blk, sub, feat = (lax.axis_index(axis) for axis in ("blk", "sub", "feat"))
    pieces = [
        forward(blk, part, blks) * subs + forward(sub, step, subs)
        for step in range(subs)
        for part in range(blks)
    ]
    turns = list(range(feats - 1, 0, -1))
    ahead = [forward(feat, step, feats) for step in [0] + turns]
    behind = [backward(feat, step, feats) for step in [0] + turns]
    places = jnp.stack(pieces + ahead + behind + [sub]).astype(jnp.int32)
    at_ahead, at_behind = len(pieces), len(pieces) + feats

    def exchange(parts):
        return [parts[0]] + [send(part, "feat", step) for part, step in zip(parts[1:], turns)]

    far, near = [blks - 1], list(range(blks - 2, 0, -1))
    other = [blks + part for part in range(blks)]
    calls = [
        [other[part] for part in far], far, [other[part] for part in near], near + [other[0]], [0], []
    ]
    plan, held, tiles = make_plan(
        target_block, source_block, slot_counts, places, sources, adjacency, calls[0]
    )
    share = None

    def local(number, after):
        nonlocal tiles, share
        turn, now, *_ = lax.optimization_barrier((plan, tiles, *after))
        taken = () if number else (places, weight, weight.shape[0] // subs)
        made, tiles, last = products(
            held, adjacency, now, turn, calls[number], calls[number + 1], blks, taken
        )
        share = last if taken else share
        return made

    others = {}
    away = local(0, [])
    shares = [fetch(share, "feat", step) for step in reversed(turns)]
    arrived = [send(value, "sub", 1) for value in away]
    kept = local(1, away)
    sums = list(pair_sum(kept, arrived))
    others.update((part, send(value, "blk", part)) for part, value in zip(far, sums))
    away = local(2, sums)
    arrived = [send(value, "sub", 1) for value in away]
    *kept, last = local(3, away)
    sums = list(pair_sum(kept, arrived))
    others.update((part, send(value, "blk", part)) for part, value in zip(near, sums))
    (kept,) = local(4, sums)
    kept, shares = lax.optimization_barrier((kept, shares))
    dealt = deal(feats, at_ahead, places, kept, [send(last, "sub", 1)] + [others[part] for part in range(1, blks)])
    dealt, shares = lax.optimization_barrier((dealt, shares))
    hidden = exchange(dealt)
    weights = [weight]
    for part in reversed(shares):
        weights += [part, send(part, "sub", 1)]
    outs = layer(at_behind, places, hidden, weights)
    return gather_rows(at_behind, places, exchange(outs))


def solution(mesh):
    return jax.shard_map(
        body,
        mesh=mesh,
        in_specs=(
            P(("blk", "sub"), "feat"),
            P(("blk", "sub"), None, None, None, None),
            P(("blk", "sub"), None, None),
            P(("blk", "sub"), None, None),
            P(("blk", "sub"), None),
            P(None, "feat"),
        ),
        out_specs=P(("blk", "sub"), "feat"),
        check_vma=False,
    )
```

```python
import functools

import jax
import jax.numpy as jnp
from jax import lax
from jax.experimental import pallas as pl
from jax.experimental.pallas import tpu as pltpu
from jax.sharding import PartitionSpec as P

TGT_DEV = 1024
GROUP = 8
PAIRS = 12
PLAN_VMEM = 45 * 2**20
PRODUCTS_VMEM = 36 * 2**20
SMALL_VMEM = 10 * 2**20


def forward(index, step, size):
    if size & (size - 1) == 0:
        return index ^ step
    return (index + step) % size


def backward(index, step, size):
    if size & (size - 1) == 0:
        return index ^ step
    return (index + size - step) % size


def send(value, axis, step):
    size = lax.axis_size(axis)
    return lax.ppermute(value, axis, [(i, forward(i, step, size)) for i in range(size)])


def fetch(value, axis, step):
    size = lax.axis_size(axis)
    return lax.ppermute(value, axis, [(forward(i, step, size), i) for i in range(size)])


def plan_sizes(slots, targets, blocks):
    rows = -(-((slots + targets) // 2) // PAIRS) * PAIRS
    return rows, slots.bit_length(), (targets - 1).bit_length(), (blocks - 1).bit_length()


class Tiles:
    def __init__(self, adj, tiles, sem, numbers, counts):
        self.adj, self.tiles, self.sem = adj, tiles, sem
        self.numbers, self.counts = numbers, counts

    def copy(self, part, group):
        some = pl.ds(group * GROUP, GROUP)
        return pltpu.make_async_copy(
            self.adj.at[0, self.numbers[part], some],
            self.tiles.at[part, some],
            self.sem.at[part, group],
        )

    def each(self, act):
        for part, count in enumerate(self.counts):

            @pl.loop(0, (count + GROUP - 1) // GROUP)
            def _(group):
                act(self.copy(part, group))

    def start(self):
        self.each(lambda copy: copy.start())
        for part in range(len(self.counts)):
            zero = jnp.zeros(self.tiles.shape[2:], self.tiles.dtype)
            self.tiles[part, self.tiles.shape[1] - 1] = zero

    def wait(self):
        self.each(lambda copy: copy.wait())


def tiles_shape(adjacency, pieces):
    slots, block = adjacency.shape[2:4]
    return jax.ShapeDtypeStruct((pieces, slots + 1, block, block), adjacency.dtype)


def tiles_sems(adjacency, pieces):
    return pltpu.SemaphoreType.DMA((pieces, adjacency.shape[2] // GROUP))


def plan_kernel(
    targets, blocks, later, ids, count, slots_ref, src_hbm, adj_hbm, out, src, tiles, sem, tile_sems
):
    large = pltpu.make_async_copy(src_hbm, src, sem)
    large.start()
    numbers = [ids[place] for place in later]
    loads = Tiles(adj_hbm, tiles, tile_sems, numbers, [count[0, number] for number in numbers])
    loads.start()
    pieces, slots = slots_ref.shape
    rows, slot_bits, target_bits, block_bits = plan_sizes(slots, targets, blocks)

    def iota(shape, axis):
        return lax.broadcasted_iota(jnp.int32, shape, axis)

    def exact(left, right):
        return jnp.dot(
            left.astype(jnp.bfloat16), right.astype(jnp.bfloat16), preferred_element_type=jnp.float32
        )

    lane = iota((1, slots), 1)
    hot, rest = [], []
    for part in range(pieces):
        piece = ids[part]
        live = lane < count[0, piece]
        both = slots_ref[pl.ds(piece, 1), :]
        target = both >> block_bits
        rest.append((live, target, both & ((1 << block_bits) - 1)))
        hot.append(((iota((targets, slots), 0) == target) & live).astype(jnp.float32))
    every = jnp.concatenate(hot, axis=0)
    before = (iota((slots, slots), 0) < iota((slots, slots), 1)).astype(jnp.float32)
    order = exact(every, before).astype(jnp.int32)
    pairs = (jnp.sum(every, axis=1, keepdims=True).astype(jnp.int32) + 1) // 2
    size = pieces * targets
    above = (iota((size, size), 1) < iota((size, size), 0)) & (
        iota((size, size), 1) // targets == iota((size, size), 0) // targets
    )
    wide = jnp.broadcast_to(pairs.astype(jnp.float32), (size, slots))
    first = exact(above.astype(jnp.float32), wide).astype(jnp.int32)
    place = every * (first + order // 2).astype(jnp.float32)
    odd = every * (order % 2).astype(jnp.float32)

    column = iota((rows, pieces), 1)
    plan = jnp.zeros((rows, pieces), jnp.int32)
    extra = jnp.zeros((8, pieces), jnp.int32)
    small = iota((8, pieces), 0)
    for part in range(pieces):
        live, target, source = rest[part]
        mine = slice(part * targets, (part + 1) * targets)
        index = jnp.sum(place[mine], axis=0, keepdims=True).astype(jnp.int32)
        second = jnp.sum(odd[mine], axis=0, keepdims=True) > 0
        hit = (iota((rows, slots), 0) == index) & live
        code = (slots - lane) | (source << slot_bits)
        one = code | (target << (slot_bits + block_bits))
        one = jnp.where(hit & jnp.logical_not(second), one.astype(jnp.float32), 0.0)
        two = jnp.where(hit & second, code.astype(jnp.float32), 0.0)
        one = jnp.sum(one, axis=1, keepdims=True).astype(jnp.int32)
        two = jnp.sum(two, axis=1, keepdims=True).astype(jnp.int32)
        both = one | (two << (slot_bits + block_bits + target_bits))
        plan = jnp.where(column == part, both, plan)
        total = jnp.sum(pairs[mine].astype(jnp.float32), axis=0, keepdims=True).astype(jnp.int32)
        values = jnp.where(small == 0, total, jnp.where(small == 1, count[0, ids[part]], ids[part]))
        extra = jnp.where(iota((8, pieces), 1) == part, values, extra)
    out[0:rows, :] = plan
    out[rows:, :] = extra
    large.wait()
    loads.wait()


def make_plan(target_block, source_block, slot_counts, places, sources, adjacency, later):
    _, pieces, slots = target_block.shape
    block = adjacency.shape[-1]
    targets, blocks = TGT_DEV // block, sources.shape[0] // block
    rows, _, _, block_bits = plan_sizes(slots, targets, blocks)
    smem, vmem, hbm = (
        pl.BlockSpec(memory_space=space) for space in (pltpu.SMEM, pltpu.VMEM, pltpu.HBM)
    )
    return pl.pallas_call(
        functools.partial(plan_kernel, targets, blocks, later),
        in_specs=[smem, smem, vmem, hbm, hbm],
        out_specs=[vmem] * 3,
        out_shape=[
            jax.ShapeDtypeStruct((rows + 8, pieces), jnp.int32),
            jax.ShapeDtypeStruct(sources.shape, sources.dtype),
            tiles_shape(adjacency, len(later)),
        ],
        scratch_shapes=[pltpu.SemaphoreType.DMA, tiles_sems(adjacency, len(later))],
        compiler_params=pltpu.CompilerParams(vmem_limit_bytes=PLAN_VMEM),
        name="plan",
    )(places, slot_counts, (target_block[0] << block_bits) + source_block[0], sources, adjacency)


def products_kernel(places, later, targets, shared, plan, src, adj, *refs):
    slots, block = adj.shape[1] - 1, adj.shape[2]
    rows, slot_bits, target_bits, block_bits = plan_sizes(slots, targets, src.shape[0] // block)
    refs = list(refs)
    if shared:
        whole, weight = refs.pop(0), refs.pop(0)
        sem, share = refs.pop(), refs.pop(-shared)
        height = share.shape[0]
        mine = pl.ds(pl.multiple_of(whole[whole.shape[0] - 1] * height, height), height)
        taking = pltpu.make_async_copy(weight.at[mine], share, sem)
        taking.start()
    if later:
        adj_hbm, *outs, tiles, acc, sems = refs
        numbers = [plan[rows + 2, place] for place in later]
        counts = [plan[rows + 1, place] for place in later]
        loads = Tiles(adj_hbm, tiles, sems, numbers, counts)
        loads.start()
    else:
        *outs, acc = refs

    def field(code, start, width):
        return (code >> start) & ((1 << width) - 1)

    def source(number):
        return src[pl.ds(pl.multiple_of(number * block, block), block), :]

    for part, out in enumerate(outs):
        total = out if out.dtype == jnp.float32 else acc
        total[...] = jnp.zeros_like(total)

        @pl.loop(0, (plan[rows, places[part]] + PAIRS - 1) // PAIRS)
        def _(step):
            for lane in range(PAIRS):
                code = plan[step * PAIRS + lane, places[part]]
                half = code >> (slot_bits + block_bits + target_bits)
                one, two = (adj[part, slots - field(c, 0, slot_bits)] for c in (code, half))
                left = jnp.concatenate([one, two], axis=1)
                one, two = (source(field(c, slot_bits, block_bits)) for c in (code, half))
                right = jnp.concatenate([one, two], axis=0)
                start = field(code, slot_bits + block_bits, target_bits) * block
                at = pl.ds(pl.multiple_of(start, block), block)
                total[at, :] += jnp.dot(left, right, preferred_element_type=jnp.float32)

        if total is acc:
            out[...] = acc[...].astype(out.dtype)
    if later:
        loads.wait()
    if shared:
        taking.wait()


def products(sources, adjacency, tiles, plan, places, later, own, taken=()):
    block = adjacency.shape[3]
    pieces = len(places)
    feat = sources.shape[1]
    smem, vmem, hbm = (
        pl.BlockSpec(memory_space=space) for space in (pltpu.SMEM, pltpu.VMEM, pltpu.HBM)
    )
    outs = [
        jax.ShapeDtypeStruct((TGT_DEV, feat), jnp.float32 if place < own else jnp.bfloat16)
        for place in places
    ]
    scratch = [pltpu.VMEM((TGT_DEV, feat), jnp.float32)]
    if later:
        outs.append(tiles_shape(adjacency, len(later)))
        scratch.append(tiles_sems(adjacency, len(later)))
    if taken:
        outs.append(jax.ShapeDtypeStruct((taken[2], taken[1].shape[1]), taken[1].dtype))
        scratch.append(pltpu.SemaphoreType.DMA)
    shared = len(scratch) if taken else 0
    got = pl.pallas_call(
        functools.partial(products_kernel, places, later, TGT_DEV // block, shared),
        in_specs=[smem, vmem, vmem] + ([smem, hbm] if taken else []) + ([hbm] if later else []),
        out_specs=[vmem] * len(outs),
        out_shape=outs,
        scratch_shapes=scratch,
        compiler_params=pltpu.CompilerParams(vmem_limit_bytes=PRODUCTS_VMEM),
        cost_estimate=pl.CostEstimate(flops=2**20, bytes_accessed=1024, transcendentals=0),
        name="products",
    )(plan, sources, tiles, *taken[:2], *([adjacency] if later else []))
    return list(got[:pieces]), (got[pieces] if later else None), got[-1]


def pair_sum_kernel(*refs):
    parts = len(refs) // 3
    for own, other, out in zip(refs[:parts], refs[parts : 2 * parts], refs[2 * parts :]):
        out[...] = (own[...] + other[...].astype(jnp.float32)).astype(out.dtype)


def pair_sum(own, others):
    vmem = pl.BlockSpec(memory_space=pltpu.VMEM)
    return pl.pallas_call(
        pair_sum_kernel,
        in_specs=[vmem] * (2 * len(own)),
        out_specs=[vmem] * len(own),
        out_shape=[jax.ShapeDtypeStruct(part.shape, jnp.bfloat16) for part in own],
        compiler_params=pltpu.CompilerParams(vmem_limit_bytes=SMALL_VMEM),
        cost_estimate=pl.CostEstimate(
            flops=own[0].size * len(own), bytes_accessed=6 * own[0].size * len(own), transcendentals=0
        ),
        name="pair_sum",
    )(*own, *others)


def deal_kernel(quarters, first, places, own, *refs):
    others, outs = refs[:-quarters], refs[-quarters:]
    rows = outs[0].shape[0]
    for quarter in range(quarters):
        here = pl.ds(pl.multiple_of(places[first + quarter] * rows, rows), rows)
        total = own[here, :]
        for other in others:
            total += other[here, :].astype(jnp.float32)
        outs[quarter][...] = total.astype(jnp.bfloat16)


def deal(quarters, first, places, own, others):
    rows, feat = own.shape
    vmem = pl.BlockSpec(memory_space=pltpu.VMEM)
    return pl.pallas_call(
        functools.partial(deal_kernel, quarters, first),
        in_specs=[pl.BlockSpec(memory_space=pltpu.SMEM)] + [vmem] * (1 + len(others)),
        out_specs=[vmem] * quarters,
        out_shape=[jax.ShapeDtypeStruct((rows // quarters, feat), jnp.bfloat16)] * quarters,
        compiler_params=pltpu.CompilerParams(vmem_limit_bytes=SMALL_VMEM),
        cost_estimate=pl.CostEstimate(
            flops=own.size * len(others), bytes_accessed=10 * own.size, transcendentals=0
        ),
        name="deal",
    )(places, own, *others)


def layer_kernel(parts, first, places, *refs):
    half = places[first + parts]
    weights, hidden = refs[: -2 * parts - 1], refs[-2 * parts - 1 : -parts - 1]
    outs = refs[-parts - 1 : -1]
    held = refs[-1]
    depth = hidden[0].shape[1]
    middle = held.shape[1] // 2
    for part, ref in enumerate(hidden):
        at = pl.multiple_of(places[first + part] * depth, depth)
        held[:, pl.ds(at, depth)] = ref[...]
    for part, out in enumerate(outs):
        if part == 0:
            total = jnp.dot(held[...], weights[0][...], preferred_element_type=jnp.float32)
        else:
            total = 0.0
            for side in range(2):
                at = pl.multiple_of((half ^ side) * middle, middle)
                share = weights[2 * part - 1 + side]
                total += jnp.dot(
                    held[:, pl.ds(at, middle)], share[...], preferred_element_type=jnp.float32
                )
        out[...] = jnp.maximum(total, 0.0).astype(out.dtype)


def layer(first, places, hidden, weights):
    parts = len(hidden)
    rows, feat = hidden[0].shape
    depth, columns = weights[0].shape
    vmem = pl.BlockSpec(memory_space=pltpu.VMEM)
    return pl.pallas_call(
        functools.partial(layer_kernel, parts, first),
        in_specs=[pl.BlockSpec(memory_space=pltpu.SMEM)] + [vmem] * (parts + len(weights)),
        out_specs=[vmem] * parts,
        out_shape=[jax.ShapeDtypeStruct((rows, columns), jnp.bfloat16)] * parts,
        scratch_shapes=[pltpu.VMEM((rows, parts * feat), jnp.bfloat16)],
        compiler_params=pltpu.CompilerParams(vmem_limit_bytes=SMALL_VMEM),
        cost_estimate=pl.CostEstimate(
            flops=2 * rows * depth * columns * parts,
            bytes_accessed=2 * parts * depth * columns,
            transcendentals=0,
        ),
        name="layer",
    )(places, *weights, *hidden)


def gather_rows_kernel(first, places, *refs):
    out = refs[-1]
    for part, piece in enumerate(refs[:-1]):
        rows = piece.shape[0]
        out[pl.ds(pl.multiple_of(places[first + part] * rows, rows), rows), :] = piece[...]


def gather_rows(first, places, pieces):
    rows, columns = pieces[0].shape
    vmem = pl.BlockSpec(memory_space=pltpu.VMEM)
    return pl.pallas_call(
        functools.partial(gather_rows_kernel, first),
        in_specs=[pl.BlockSpec(memory_space=pltpu.SMEM)] + [vmem] * len(pieces),
        out_specs=vmem,
        out_shape=jax.ShapeDtypeStruct((rows * len(pieces), columns), pieces[0].dtype),
        compiler_params=pltpu.CompilerParams(vmem_limit_bytes=SMALL_VMEM),
        name="gather_rows",
    )(places, *pieces)


def body(sources, adjacency, target_block, source_block, slot_counts, weight):
    blks, subs, feats = (lax.axis_size(axis) for axis in ("blk", "sub", "feat"))
    blk, sub, feat = (lax.axis_index(axis) for axis in ("blk", "sub", "feat"))
    pieces = [
        forward(blk, part, blks) * subs + forward(sub, step, subs)
        for step in range(subs)
        for part in range(blks)
    ]
    turns = list(range(feats - 1, 0, -1))
    ahead = [forward(feat, step, feats) for step in [0] + turns]
    behind = [backward(feat, step, feats) for step in [0] + turns]
    places = jnp.stack(pieces + ahead + behind + [sub]).astype(jnp.int32)
    at_ahead, at_behind = len(pieces), len(pieces) + feats

    def exchange(parts):
        return [parts[0]] + [send(part, "feat", step) for part, step in zip(parts[1:], turns)]

    far, near = [blks - 1], list(range(blks - 2, 0, -1))
    other = [blks + part for part in range(blks)]
    calls = [
        [other[part] for part in far], far, [other[part] for part in near], near + [other[0]], [0], []
    ]
    plan, held, tiles = make_plan(
        target_block, source_block, slot_counts, places, sources, adjacency, calls[0]
    )
    share = None

    def local(number, after):
        nonlocal tiles, share
        turn, now, *_ = lax.optimization_barrier((plan, tiles, *after))
        taken = () if number else (places, weight, weight.shape[0] // subs)
        made, tiles, last = products(
            held, adjacency, now, turn, calls[number], calls[number + 1], blks, taken
        )
        share = last if taken else share
        return made

    others = {}
    away = local(0, [])
    shares = [fetch(share, "feat", step) for step in reversed(turns)]
    arrived = [send(value, "sub", 1) for value in away]
    kept = local(1, away)
    sums = list(pair_sum(kept, arrived))
    others.update((part, send(value, "blk", part)) for part, value in zip(far, sums))
    away = local(2, sums)
    arrived = [send(value, "sub", 1) for value in away]
    *kept, last = local(3, away)
    sums = list(pair_sum(kept, arrived))
    others.update((part, send(value, "blk", part)) for part, value in zip(near, sums))
    (kept,) = local(4, sums)
    kept, shares = lax.optimization_barrier((kept, shares))
    dealt = deal(feats, at_ahead, places, kept, [send(last, "sub", 1)] + [others[part] for part in range(1, blks)])
    dealt, shares = lax.optimization_barrier((dealt, shares))
    hidden = exchange(dealt)
    weights = [weight]
    for part in reversed(shares):
        weights += [part, send(part, "sub", 1)]
    outs = layer(at_behind, places, hidden, weights)
    return gather_rows(at_behind, places, exchange(outs))


def solution(mesh):
    return jax.shard_map(
        body,
        mesh=mesh,
        in_specs=(
            P(("blk", "sub"), "feat"),
            P(("blk", "sub"), None, None, None, None),
            P(("blk", "sub"), None, None),
            P(("blk", "sub"), None, None),
            P(("blk", "sub"), None),
            P(None, "feat"),
        ),
        out_specs=P(("blk", "sub"), "feat"),
        check_vma=False,
    )
```

```python
import functools

import jax
import jax.numpy as jnp
from jax import lax
from jax.experimental import pallas as pl
from jax.experimental.pallas import tpu as pltpu
from jax.sharding import PartitionSpec as P

TGT_DEV = 1024
GROUP = 8
PAIRS = 12
PLAN_VMEM = 45 * 2**20
PRODUCTS_VMEM = 36 * 2**20
SMALL_VMEM = 10 * 2**20


def forward(index, step, size):
    if size & (size - 1) == 0:
        return index ^ step
    return (index + step) % size


def backward(index, step, size):
    if size & (size - 1) == 0:
        return index ^ step
    return (index + size - step) % size


def send(value, axis, step):
    size = lax.axis_size(axis)
    return lax.ppermute(value, axis, [(i, forward(i, step, size)) for i in range(size)])


def fetch(value, axis, step):
    size = lax.axis_size(axis)
    return lax.ppermute(value, axis, [(forward(i, step, size), i) for i in range(size)])


def plan_sizes(slots, targets, blocks):
    rows = -(-((slots + targets) // 2) // PAIRS) * PAIRS
    return rows, slots.bit_length(), (targets - 1).bit_length(), (blocks - 1).bit_length()


class Tiles:
    def __init__(self, adj, tiles, sem, numbers, counts):
        self.adj, self.tiles, self.sem = adj, tiles, sem
        self.numbers, self.counts = numbers, counts

    def copy(self, part, group):
        some = pl.ds(group * GROUP, GROUP)
        return pltpu.make_async_copy(
            self.adj.at[0, self.numbers[part], some],
            self.tiles.at[part, some],
            self.sem.at[part, group],
        )

    def each(self, act):
        for part, count in enumerate(self.counts):

            @pl.loop(0, (count + GROUP - 1) // GROUP)
            def _(group):
                act(self.copy(part, group))

    def start(self):
        self.each(lambda copy: copy.start())
        for part in range(len(self.counts)):
            zero = jnp.zeros(self.tiles.shape[2:], self.tiles.dtype)
            self.tiles[part, self.tiles.shape[1] - 1] = zero

    def wait(self):
        self.each(lambda copy: copy.wait())


def tiles_shape(adjacency, pieces):
    slots, block = adjacency.shape[2:4]
    return jax.ShapeDtypeStruct((pieces, slots + 1, block, block), adjacency.dtype)


def tiles_sems(adjacency, pieces):
    return pltpu.SemaphoreType.DMA((pieces, adjacency.shape[2] // GROUP))


def plan_kernel(
    targets, blocks, later, ids, count, slots_ref, src_hbm, adj_hbm, out, src, tiles, sem, tile_sems
):
    large = pltpu.make_async_copy(src_hbm, src, sem)
    large.start()
    numbers = [ids[place] for place in later]
    loads = Tiles(adj_hbm, tiles, tile_sems, numbers, [count[0, number] for number in numbers])
    loads.start()
    pieces, slots = slots_ref.shape
    rows, slot_bits, target_bits, block_bits = plan_sizes(slots, targets, blocks)

    def iota(shape, axis):
        return lax.broadcasted_iota(jnp.int32, shape, axis)

    def exact(left, right):
        return jnp.dot(
            left.astype(jnp.bfloat16), right.astype(jnp.bfloat16), preferred_element_type=jnp.float32
        )

    lane = iota((1, slots), 1)
    hot, rest = [], []
    for part in range(pieces):
        piece = ids[part]
        live = lane < count[0, piece]
        both = slots_ref[pl.ds(piece, 1), :]
        target = both >> block_bits
        rest.append((live, target, both & ((1 << block_bits) - 1)))
        hot.append(((iota((targets, slots), 0) == target) & live).astype(jnp.float32))
    every = jnp.concatenate(hot, axis=0)
    before = (iota((slots, slots), 0) < iota((slots, slots), 1)).astype(jnp.float32)
    order = exact(every, before).astype(jnp.int32)
    pairs = (jnp.sum(every, axis=1, keepdims=True).astype(jnp.int32) + 1) // 2
    size = pieces * targets
    above = (iota((size, size), 1) < iota((size, size), 0)) & (
        iota((size, size), 1) // targets == iota((size, size), 0) // targets
    )
    wide = jnp.broadcast_to(pairs.astype(jnp.float32), (size, slots))
    first = exact(above.astype(jnp.float32), wide).astype(jnp.int32)
    place = every * (first + order // 2).astype(jnp.float32)
    odd = every * (order % 2).astype(jnp.float32)

    column = iota((rows, pieces), 1)
    plan = jnp.zeros((rows, pieces), jnp.int32)
    extra = jnp.zeros((8, pieces), jnp.int32)
    small = iota((8, pieces), 0)
    for part in range(pieces):
        live, target, source = rest[part]
        mine = slice(part * targets, (part + 1) * targets)
        index = jnp.sum(place[mine], axis=0, keepdims=True).astype(jnp.int32)
        second = jnp.sum(odd[mine], axis=0, keepdims=True) > 0
        hit = (iota((rows, slots), 0) == index) & live
        code = (slots - lane) | (source << slot_bits)
        one = code | (target << (slot_bits + block_bits))
        one = jnp.where(hit & jnp.logical_not(second), one.astype(jnp.float32), 0.0)
        two = jnp.where(hit & second, code.astype(jnp.float32), 0.0)
        one = jnp.sum(one, axis=1, keepdims=True).astype(jnp.int32)
        two = jnp.sum(two, axis=1, keepdims=True).astype(jnp.int32)
        both = one | (two << (slot_bits + block_bits + target_bits))
        plan = jnp.where(column == part, both, plan)
        total = jnp.sum(pairs[mine].astype(jnp.float32), axis=0, keepdims=True).astype(jnp.int32)
        values = jnp.where(small == 0, total, jnp.where(small == 1, count[0, ids[part]], ids[part]))
        extra = jnp.where(iota((8, pieces), 1) == part, values, extra)
    out[0:rows, :] = plan
    out[rows:, :] = extra
    large.wait()
    loads.wait()


def make_plan(target_block, source_block, slot_counts, places, sources, adjacency, later):
    _, pieces, slots = target_block.shape
    block = adjacency.shape[-1]
    targets, blocks = TGT_DEV // block, sources.shape[0] // block
    rows, _, _, block_bits = plan_sizes(slots, targets, blocks)
    smem, vmem, hbm = (
        pl.BlockSpec(memory_space=space) for space in (pltpu.SMEM, pltpu.VMEM, pltpu.HBM)
    )
    return pl.pallas_call(
        functools.partial(plan_kernel, targets, blocks, later),
        in_specs=[smem, smem, vmem, hbm, hbm],
        out_specs=[vmem] * 3,
        out_shape=[
            jax.ShapeDtypeStruct((rows + 8, pieces), jnp.int32),
            jax.ShapeDtypeStruct(sources.shape, sources.dtype),
            tiles_shape(adjacency, len(later)),
        ],
        scratch_shapes=[pltpu.SemaphoreType.DMA, tiles_sems(adjacency, len(later))],
        compiler_params=pltpu.CompilerParams(vmem_limit_bytes=PLAN_VMEM),
        name="plan",
    )(places, slot_counts, (target_block[0] << block_bits) + source_block[0], sources, adjacency)


def products_kernel(places, later, targets, shared, plan, src, adj, *refs):
    slots, block = adj.shape[1] - 1, adj.shape[2]
    rows, slot_bits, target_bits, block_bits = plan_sizes(slots, targets, src.shape[0] // block)
    refs = list(refs)
    if shared:
        whole, weight = refs.pop(0), refs.pop(0)
        sem, share = refs.pop(), refs.pop(-shared)
        height = share.shape[0]
        mine = pl.ds(pl.multiple_of(whole[whole.shape[0] - 1] * height, height), height)
        taking = pltpu.make_async_copy(weight.at[mine], share, sem)
        taking.start()
    if later:
        adj_hbm, *outs, tiles, acc, sems = refs
        numbers = [plan[rows + 2, place] for place in later]
        counts = [plan[rows + 1, place] for place in later]
        loads = Tiles(adj_hbm, tiles, sems, numbers, counts)
        loads.start()
    else:
        *outs, acc = refs

    def field(code, start, width):
        return (code >> start) & ((1 << width) - 1)

    def source(number):
        return src[pl.ds(pl.multiple_of(number * block, block), block), :]

    for part, out in enumerate(outs):
        total = out if out.dtype == jnp.float32 else acc
        total[...] = jnp.zeros_like(total)

        @pl.loop(0, (plan[rows, places[part]] + PAIRS - 1) // PAIRS)
        def _(step):
            for lane in range(PAIRS):
                code = plan[step * PAIRS + lane, places[part]]
                half = code >> (slot_bits + block_bits + target_bits)
                one, two = (adj[part, slots - field(c, 0, slot_bits)] for c in (code, half))
                left = jnp.concatenate([one, two], axis=1)
                one, two = (source(field(c, slot_bits, block_bits)) for c in (code, half))
                right = jnp.concatenate([one, two], axis=0)
                start = field(code, slot_bits + block_bits, target_bits) * block
                at = pl.ds(pl.multiple_of(start, block), block)
                total[at, :] += jnp.dot(left, right, preferred_element_type=jnp.float32)

        if total is acc:
            out[...] = acc[...].astype(out.dtype)
    if later:
        loads.wait()
    if shared:
        taking.wait()


def products(sources, adjacency, tiles, plan, places, later, own, taken=()):
    block = adjacency.shape[3]
    pieces = len(places)
    feat = sources.shape[1]
    smem, vmem, hbm = (
        pl.BlockSpec(memory_space=space) for space in (pltpu.SMEM, pltpu.VMEM, pltpu.HBM)
    )
    outs = [
        jax.ShapeDtypeStruct((TGT_DEV, feat), jnp.float32 if place < own else jnp.bfloat16)
        for place in places
    ]
    scratch = [pltpu.VMEM((TGT_DEV, feat), jnp.float32)]
    if later:
        outs.append(tiles_shape(adjacency, len(later)))
        scratch.append(tiles_sems(adjacency, len(later)))
    if taken:
        outs.append(jax.ShapeDtypeStruct((taken[2], taken[1].shape[1]), taken[1].dtype))
        scratch.append(pltpu.SemaphoreType.DMA)
    shared = len(scratch) if taken else 0
    got = pl.pallas_call(
        functools.partial(products_kernel, places, later, TGT_DEV // block, shared),
        in_specs=[smem, vmem, vmem] + ([smem, hbm] if taken else []) + ([hbm] if later else []),
        out_specs=[vmem] * len(outs),
        out_shape=outs,
        scratch_shapes=scratch,
        compiler_params=pltpu.CompilerParams(vmem_limit_bytes=PRODUCTS_VMEM),
        cost_estimate=pl.CostEstimate(flops=2**20, bytes_accessed=1024, transcendentals=0),
        name="products",
    )(plan, sources, tiles, *taken[:2], *([adjacency] if later else []))
    return list(got[:pieces]), (got[pieces] if later else None), got[-1]


def pair_sum_kernel(*refs):
    parts = len(refs) // 3
    for own, other, out in zip(refs[:parts], refs[parts : 2 * parts], refs[2 * parts :]):
        out[...] = (own[...] + other[...].astype(jnp.float32)).astype(out.dtype)


def pair_sum(own, others):
    vmem = pl.BlockSpec(memory_space=pltpu.VMEM)
    return pl.pallas_call(
        pair_sum_kernel,
        in_specs=[vmem] * (2 * len(own)),
        out_specs=[vmem] * len(own),
        out_shape=[jax.ShapeDtypeStruct(part.shape, jnp.bfloat16) for part in own],
        compiler_params=pltpu.CompilerParams(vmem_limit_bytes=SMALL_VMEM),
        cost_estimate=pl.CostEstimate(
            flops=own[0].size * len(own), bytes_accessed=6 * own[0].size * len(own), transcendentals=0
        ),
        name="pair_sum",
    )(*own, *others)


def deal_kernel(quarters, first, places, own, *refs):
    others, outs = refs[:-quarters], refs[-quarters:]
    rows = outs[0].shape[0]
    for quarter in range(quarters):
        here = pl.ds(pl.multiple_of(places[first + quarter] * rows, rows), rows)
        total = own[here, :]
        for other in others:
            total += other[here, :].astype(jnp.float32)
        outs[quarter][...] = total.astype(jnp.bfloat16)


def deal(quarters, first, places, own, others):
    rows, feat = own.shape
    vmem = pl.BlockSpec(memory_space=pltpu.VMEM)
    return pl.pallas_call(
        functools.partial(deal_kernel, quarters, first),
        in_specs=[pl.BlockSpec(memory_space=pltpu.SMEM)] + [vmem] * (1 + len(others)),
        out_specs=[vmem] * quarters,
        out_shape=[jax.ShapeDtypeStruct((rows // quarters, feat), jnp.bfloat16)] * quarters,
        compiler_params=pltpu.CompilerParams(vmem_limit_bytes=SMALL_VMEM),
        cost_estimate=pl.CostEstimate(
            flops=own.size * len(others), bytes_accessed=10 * own.size, transcendentals=0
        ),
        name="deal",
    )(places, own, *others)


def layer_kernel(parts, first, places, *refs):
    half = places[first + parts]
    weights, hidden = refs[: -2 * parts - 1], refs[-2 * parts - 1 : -parts - 1]
    outs = refs[-parts - 1 : -1]
    held = refs[-1]
    depth = hidden[0].shape[1]
    middle = held.shape[1] // 2
    for part, ref in enumerate(hidden):
        at = pl.multiple_of(places[first + part] * depth, depth)
        held[:, pl.ds(at, depth)] = ref[...]
    for part, out in enumerate(outs):
        if part == 0:
            total = jnp.dot(held[...], weights[0][...], preferred_element_type=jnp.float32)
        else:
            total = 0.0
            for side in range(2):
                at = pl.multiple_of((half ^ side) * middle, middle)
                share = weights[2 * part - 1 + side]
                total += jnp.dot(
                    held[:, pl.ds(at, middle)], share[...], preferred_element_type=jnp.float32
                )
        out[...] = jnp.maximum(total, 0.0).astype(out.dtype)


def layer(first, places, hidden, weights):
    parts = len(hidden)
    rows, feat = hidden[0].shape
    depth, columns = weights[0].shape
    vmem = pl.BlockSpec(memory_space=pltpu.VMEM)
    return pl.pallas_call(
        functools.partial(layer_kernel, parts, first),
        in_specs=[pl.BlockSpec(memory_space=pltpu.SMEM)] + [vmem] * (parts + len(weights)),
        out_specs=[vmem] * parts,
        out_shape=[jax.ShapeDtypeStruct((rows, columns), jnp.bfloat16)] * parts,
        scratch_shapes=[pltpu.VMEM((rows, parts * feat), jnp.bfloat16)],
        compiler_params=pltpu.CompilerParams(vmem_limit_bytes=SMALL_VMEM),
        cost_estimate=pl.CostEstimate(
            flops=2 * rows * depth * columns * parts,
            bytes_accessed=2 * parts * depth * columns,
            transcendentals=0,
        ),
        name="layer",
    )(places, *weights, *hidden)


def gather_rows_kernel(first, places, *refs):
    out = refs[-1]
    for part, piece in enumerate(refs[:-1]):
        rows = piece.shape[0]
        out[pl.ds(pl.multiple_of(places[first + part] * rows, rows), rows), :] = piece[...]


def gather_rows(first, places, pieces):
    rows, columns = pieces[0].shape
    vmem = pl.BlockSpec(memory_space=pltpu.VMEM)
    return pl.pallas_call(
        functools.partial(gather_rows_kernel, first),
        in_specs=[pl.BlockSpec(memory_space=pltpu.SMEM)] + [vmem] * len(pieces),
        out_specs=vmem,
        out_shape=jax.ShapeDtypeStruct((rows * len(pieces), columns), pieces[0].dtype),
        compiler_params=pltpu.CompilerParams(vmem_limit_bytes=SMALL_VMEM),
        name="gather_rows",
    )(places, *pieces)


def body(sources, adjacency, target_block, source_block, slot_counts, weight):
    blks, subs, feats = (lax.axis_size(axis) for axis in ("blk", "sub", "feat"))
    blk, sub, feat = (lax.axis_index(axis) for axis in ("blk", "sub", "feat"))
    pieces = [
        forward(blk, part, blks) * subs + forward(sub, step, subs)
        for step in range(subs)
        for part in range(blks)
    ]
    turns = list(range(feats - 1, 0, -1))
    ahead = [forward(feat, step, feats) for step in [0] + turns]
    behind = [backward(feat, step, feats) for step in [0] + turns]
    places = jnp.stack(pieces + ahead + behind + [sub]).astype(jnp.int32)
    at_ahead, at_behind = len(pieces), len(pieces) + feats

    def exchange(parts):
        return [parts[0]] + [send(part, "feat", step) for part, step in zip(parts[1:], turns)]

    far, near = [blks - 1], list(range(blks - 2, 0, -1))
    other = [blks + part for part in range(blks)]
    calls = [
        [other[part] for part in far], far, [other[part] for part in near], [other[0]] + near, [0], []
    ]
    plan, held, tiles = make_plan(
        target_block, source_block, slot_counts, places, sources, adjacency, calls[0]
    )
    share = None

    def local(number, after):
        nonlocal tiles, share
        turn, now, *_ = lax.optimization_barrier((plan, tiles, *after))
        taken = () if number else (places, weight, weight.shape[0] // subs)
        made, tiles, last = products(
            held, adjacency, now, turn, calls[number], calls[number + 1], blks, taken
        )
        share = last if taken else share
        return made

    others = {}
    away = local(0, [])
    shares = [fetch(share, "feat", step) for step in reversed(turns)]
    arrived = [send(value, "sub", 1) for value in away]
    kept = local(1, away)
    sums = list(pair_sum(kept, arrived))
    others.update((part, send(value, "blk", part)) for part, value in zip(far, sums))
    away = local(2, sums)
    arrived = [send(value, "sub", 1) for value in away]
    last, *kept = local(3, away)
    sums = list(pair_sum(kept, arrived))
    others.update((part, send(value, "blk", part)) for part, value in zip(near, sums))
    (kept,) = local(4, sums)
    kept, shares = lax.optimization_barrier((kept, shares))
    dealt = deal(feats, at_ahead, places, kept, [send(last, "sub", 1)] + [others[part] for part in range(1, blks)])
    dealt, shares = lax.optimization_barrier((dealt, shares))
    hidden = exchange(dealt)
    weights = [weight]
    for part in reversed(shares):
        weights += [part, send(part, "sub", 1)]
    outs = layer(at_behind, places, hidden, weights)
    return gather_rows(at_behind, places, exchange(outs))


def solution(mesh):
    return jax.shard_map(
        body,
        mesh=mesh,
        in_specs=(
            P(("blk", "sub"), "feat"),
            P(("blk", "sub"), None, None, None, None),
            P(("blk", "sub"), None, None),
            P(("blk", "sub"), None, None),
            P(("blk", "sub"), None),
            P(None, "feat"),
        ),
        out_specs=P(("blk", "sub"), "feat"),
        check_vma=False,
    )
```

```python
import functools

import jax
import jax.numpy as jnp
from jax import lax
from jax.experimental import pallas as pl
from jax.experimental.pallas import tpu as pltpu
from jax.sharding import PartitionSpec as P

TGT_DEV = 1024
GROUP = 8
PAIRS = 18
PLAN_VMEM = 45 * 2**20
PRODUCTS_VMEM = 36 * 2**20
SMALL_VMEM = 10 * 2**20


def forward(index, step, size):
    if size & (size - 1) == 0:
        return index ^ step
    return (index + step) % size


def backward(index, step, size):
    if size & (size - 1) == 0:
        return index ^ step
    return (index + size - step) % size


def send(value, axis, step):
    size = lax.axis_size(axis)
    return lax.ppermute(value, axis, [(i, forward(i, step, size)) for i in range(size)])


def fetch(value, axis, step):
    size = lax.axis_size(axis)
    return lax.ppermute(value, axis, [(forward(i, step, size), i) for i in range(size)])


def plan_sizes(slots, targets, blocks):
    rows = -(-((slots + targets) // 2) // PAIRS) * PAIRS
    return rows, slots.bit_length(), (targets - 1).bit_length(), (blocks - 1).bit_length()


class Tiles:
    def __init__(self, adj, tiles, sem, numbers, counts):
        self.adj, self.tiles, self.sem = adj, tiles, sem
        self.numbers, self.counts = numbers, counts

    def copy(self, part, group):
        some = pl.ds(group * GROUP, GROUP)
        return pltpu.make_async_copy(
            self.adj.at[0, self.numbers[part], some],
            self.tiles.at[part, some],
            self.sem.at[part, group],
        )

    def each(self, act):
        for part, count in enumerate(self.counts):

            @pl.loop(0, (count + GROUP - 1) // GROUP)
            def _(group):
                act(self.copy(part, group))

    def start(self):
        self.each(lambda copy: copy.start())
        for part in range(len(self.counts)):
            zero = jnp.zeros(self.tiles.shape[2:], self.tiles.dtype)
            self.tiles[part, self.tiles.shape[1] - 1] = zero

    def wait(self):
        self.each(lambda copy: copy.wait())


def tiles_shape(adjacency, pieces):
    slots, block = adjacency.shape[2:4]
    return jax.ShapeDtypeStruct((pieces, slots + 1, block, block), adjacency.dtype)


def tiles_sems(adjacency, pieces):
    return pltpu.SemaphoreType.DMA((pieces, adjacency.shape[2] // GROUP))


def plan_kernel(
    targets, blocks, later, ids, count, slots_ref, src_hbm, adj_hbm, out, src, tiles, sem, tile_sems
):
    large = pltpu.make_async_copy(src_hbm, src, sem)
    large.start()
    numbers = [ids[place] for place in later]
    loads = Tiles(adj_hbm, tiles, tile_sems, numbers, [count[0, number] for number in numbers])
    loads.start()
    pieces, slots = slots_ref.shape
    rows, slot_bits, target_bits, block_bits = plan_sizes(slots, targets, blocks)

    def iota(shape, axis):
        return lax.broadcasted_iota(jnp.int32, shape, axis)

    def exact(left, right):
        return jnp.dot(
            left.astype(jnp.bfloat16), right.astype(jnp.bfloat16), preferred_element_type=jnp.float32
        )

    lane = iota((1, slots), 1)
    hot, rest = [], []
    for part in range(pieces):
        piece = ids[part]
        live = lane < count[0, piece]
        both = slots_ref[pl.ds(piece, 1), :]
        target = both >> block_bits
        rest.append((live, target, both & ((1 << block_bits) - 1)))
        hot.append(((iota((targets, slots), 0) == target) & live).astype(jnp.float32))
    every = jnp.concatenate(hot, axis=0)
    before = (iota((slots, slots), 0) < iota((slots, slots), 1)).astype(jnp.float32)
    order = exact(every, before).astype(jnp.int32)
    pairs = (jnp.sum(every, axis=1, keepdims=True).astype(jnp.int32) + 1) // 2
    size = pieces * targets
    above = (iota((size, size), 1) < iota((size, size), 0)) & (
        iota((size, size), 1) // targets == iota((size, size), 0) // targets
    )
    wide = jnp.broadcast_to(pairs.astype(jnp.float32), (size, slots))
    first = exact(above.astype(jnp.float32), wide).astype(jnp.int32)
    place = every * (first + order // 2).astype(jnp.float32)
    odd = every * (order % 2).astype(jnp.float32)

    column = iota((rows, pieces), 1)
    plan = jnp.zeros((rows, pieces), jnp.int32)
    extra = jnp.zeros((8, pieces), jnp.int32)
    small = iota((8, pieces), 0)
    for part in range(pieces):
        live, target, source = rest[part]
        mine = slice(part * targets, (part + 1) * targets)
        index = jnp.sum(place[mine], axis=0, keepdims=True).astype(jnp.int32)
        second = jnp.sum(odd[mine], axis=0, keepdims=True) > 0
        hit = (iota((rows, slots), 0) == index) & live
        code = (slots - lane) | (source << slot_bits)
        one = code | (target << (slot_bits + block_bits))
        one = jnp.where(hit & jnp.logical_not(second), one.astype(jnp.float32), 0.0)
        two = jnp.where(hit & second, code.astype(jnp.float32), 0.0)
        one = jnp.sum(one, axis=1, keepdims=True).astype(jnp.int32)
        two = jnp.sum(two, axis=1, keepdims=True).astype(jnp.int32)
        both = one | (two << (slot_bits + block_bits + target_bits))
        plan = jnp.where(column == part, both, plan)
        total = jnp.sum(pairs[mine].astype(jnp.float32), axis=0, keepdims=True).astype(jnp.int32)
        values = jnp.where(small == 0, total, jnp.where(small == 1, count[0, ids[part]], ids[part]))
        extra = jnp.where(iota((8, pieces), 1) == part, values, extra)
    out[0:rows, :] = plan
    out[rows:, :] = extra
    large.wait()
    loads.wait()


def make_plan(target_block, source_block, slot_counts, places, sources, adjacency, later):
    _, pieces, slots = target_block.shape
    block = adjacency.shape[-1]
    targets, blocks = TGT_DEV // block, sources.shape[0] // block
    rows, _, _, block_bits = plan_sizes(slots, targets, blocks)
    smem, vmem, hbm = (
        pl.BlockSpec(memory_space=space) for space in (pltpu.SMEM, pltpu.VMEM, pltpu.HBM)
    )
    return pl.pallas_call(
        functools.partial(plan_kernel, targets, blocks, later),
        in_specs=[smem, smem, vmem, hbm, hbm],
        out_specs=[vmem] * 3,
        out_shape=[
            jax.ShapeDtypeStruct((rows + 8, pieces), jnp.int32),
            jax.ShapeDtypeStruct(sources.shape, sources.dtype),
            tiles_shape(adjacency, len(later)),
        ],
        scratch_shapes=[pltpu.SemaphoreType.DMA, tiles_sems(adjacency, len(later))],
        compiler_params=pltpu.CompilerParams(vmem_limit_bytes=PLAN_VMEM),
        name="plan",
    )(places, slot_counts, (target_block[0] << block_bits) + source_block[0], sources, adjacency)


def products_kernel(places, later, targets, shared, plan, src, adj, *refs):
    slots, block = adj.shape[1] - 1, adj.shape[2]
    rows, slot_bits, target_bits, block_bits = plan_sizes(slots, targets, src.shape[0] // block)
    refs = list(refs)
    if shared:
        whole, weight = refs.pop(0), refs.pop(0)
        sem, share = refs.pop(), refs.pop(-shared)
        height = share.shape[0]
        mine = pl.ds(pl.multiple_of(whole[whole.shape[0] - 1] * height, height), height)
        taking = pltpu.make_async_copy(weight.at[mine], share, sem)
        taking.start()
    if later:
        adj_hbm, *outs, tiles, acc, sems = refs
        numbers = [plan[rows + 2, place] for place in later]
        counts = [plan[rows + 1, place] for place in later]
        loads = Tiles(adj_hbm, tiles, sems, numbers, counts)
        loads.start()
    else:
        *outs, acc = refs

    def field(code, start, width):
        return (code >> start) & ((1 << width) - 1)

    def source(number):
        return src[pl.ds(pl.multiple_of(number * block, block), block), :]

    for part, out in enumerate(outs):
        total = out if out.dtype == jnp.float32 else acc
        total[...] = jnp.zeros_like(total)

        @pl.loop(0, (plan[rows, places[part]] + PAIRS - 1) // PAIRS)
        def _(step):
            for lane in range(PAIRS):
                code = plan[step * PAIRS + lane, places[part]]
                half = code >> (slot_bits + block_bits + target_bits)
                one, two = (adj[part, slots - field(c, 0, slot_bits)] for c in (code, half))
                left = jnp.concatenate([one, two], axis=1)
                one, two = (source(field(c, slot_bits, block_bits)) for c in (code, half))
                right = jnp.concatenate([one, two], axis=0)
                start = field(code, slot_bits + block_bits, target_bits) * block
                at = pl.ds(pl.multiple_of(start, block), block)
                total[at, :] += jnp.dot(left, right, preferred_element_type=jnp.float32)

        if total is acc:
            out[...] = acc[...].astype(out.dtype)
    if later:
        loads.wait()
    if shared:
        taking.wait()


def products(sources, adjacency, tiles, plan, places, later, own, taken=()):
    block = adjacency.shape[3]
    pieces = len(places)
    feat = sources.shape[1]
    smem, vmem, hbm = (
        pl.BlockSpec(memory_space=space) for space in (pltpu.SMEM, pltpu.VMEM, pltpu.HBM)
    )
    outs = [
        jax.ShapeDtypeStruct((TGT_DEV, feat), jnp.float32 if place < own else jnp.bfloat16)
        for place in places
    ]
    scratch = [pltpu.VMEM((TGT_DEV, feat), jnp.float32)]
    if later:
        outs.append(tiles_shape(adjacency, len(later)))
        scratch.append(tiles_sems(adjacency, len(later)))
    if taken:
        outs.append(jax.ShapeDtypeStruct((taken[2], taken[1].shape[1]), taken[1].dtype))
        scratch.append(pltpu.SemaphoreType.DMA)
    shared = len(scratch) if taken else 0
    got = pl.pallas_call(
        functools.partial(products_kernel, places, later, TGT_DEV // block, shared),
        in_specs=[smem, vmem, vmem] + ([smem, hbm] if taken else []) + ([hbm] if later else []),
        out_specs=[vmem] * len(outs),
        out_shape=outs,
        scratch_shapes=scratch,
        compiler_params=pltpu.CompilerParams(vmem_limit_bytes=PRODUCTS_VMEM),
        cost_estimate=pl.CostEstimate(flops=2**20, bytes_accessed=1024, transcendentals=0),
        name="products",
    )(plan, sources, tiles, *taken[:2], *([adjacency] if later else []))
    return list(got[:pieces]), (got[pieces] if later else None), got[-1]


def pair_sum_kernel(*refs):
    parts = len(refs) // 3
    for own, other, out in zip(refs[:parts], refs[parts : 2 * parts], refs[2 * parts :]):
        out[...] = (own[...] + other[...].astype(jnp.float32)).astype(out.dtype)


def pair_sum(own, others):
    vmem = pl.BlockSpec(memory_space=pltpu.VMEM)
    return pl.pallas_call(
        pair_sum_kernel,
        in_specs=[vmem] * (2 * len(own)),
        out_specs=[vmem] * len(own),
        out_shape=[jax.ShapeDtypeStruct(part.shape, jnp.bfloat16) for part in own],
        compiler_params=pltpu.CompilerParams(vmem_limit_bytes=SMALL_VMEM),
        cost_estimate=pl.CostEstimate(
            flops=own[0].size * len(own), bytes_accessed=6 * own[0].size * len(own), transcendentals=0
        ),
        name="pair_sum",
    )(*own, *others)


def deal_kernel(quarters, first, places, own, *refs):
    others, outs = refs[:-quarters], refs[-quarters:]
    rows = outs[0].shape[0]
    for quarter in range(quarters):
        here = pl.ds(pl.multiple_of(places[first + quarter] * rows, rows), rows)
        total = own[here, :]
        for other in others:
            total += other[here, :].astype(jnp.float32)
        outs[quarter][...] = total.astype(jnp.bfloat16)


def deal(quarters, first, places, own, others):
    rows, feat = own.shape
    vmem = pl.BlockSpec(memory_space=pltpu.VMEM)
    return pl.pallas_call(
        functools.partial(deal_kernel, quarters, first),
        in_specs=[pl.BlockSpec(memory_space=pltpu.SMEM)] + [vmem] * (1 + len(others)),
        out_specs=[vmem] * quarters,
        out_shape=[jax.ShapeDtypeStruct((rows // quarters, feat), jnp.bfloat16)] * quarters,
        compiler_params=pltpu.CompilerParams(vmem_limit_bytes=SMALL_VMEM),
        cost_estimate=pl.CostEstimate(
            flops=own.size * len(others), bytes_accessed=10 * own.size, transcendentals=0
        ),
        name="deal",
    )(places, own, *others)


def layer_kernel(parts, first, places, *refs):
    half = places[first + parts]
    weights, hidden = refs[: -2 * parts - 1], refs[-2 * parts - 1 : -parts - 1]
    outs = refs[-parts - 1 : -1]
    held = refs[-1]
    depth = hidden[0].shape[1]
    middle = held.shape[1] // 2
    for part, ref in enumerate(hidden):
        at = pl.multiple_of(places[first + part] * depth, depth)
        held[:, pl.ds(at, depth)] = ref[...]
    for part, out in enumerate(outs):
        if part == 0:
            total = jnp.dot(held[...], weights[0][...], preferred_element_type=jnp.float32)
        else:
            total = 0.0
            for side in range(2):
                at = pl.multiple_of((half ^ side) * middle, middle)
                share = weights[2 * part - 1 + side]
                total += jnp.dot(
                    held[:, pl.ds(at, middle)], share[...], preferred_element_type=jnp.float32
                )
        out[...] = jnp.maximum(total, 0.0).astype(out.dtype)


def layer(first, places, hidden, weights):
    parts = len(hidden)
    rows, feat = hidden[0].shape
    depth, columns = weights[0].shape
    vmem = pl.BlockSpec(memory_space=pltpu.VMEM)
    return pl.pallas_call(
        functools.partial(layer_kernel, parts, first),
        in_specs=[pl.BlockSpec(memory_space=pltpu.SMEM)] + [vmem] * (parts + len(weights)),
        out_specs=[vmem] * parts,
        out_shape=[jax.ShapeDtypeStruct((rows, columns), jnp.bfloat16)] * parts,
        scratch_shapes=[pltpu.VMEM((rows, parts * feat), jnp.bfloat16)],
        compiler_params=pltpu.CompilerParams(vmem_limit_bytes=SMALL_VMEM),
        cost_estimate=pl.CostEstimate(
            flops=2 * rows * depth * columns * parts,
            bytes_accessed=2 * parts * depth * columns,
            transcendentals=0,
        ),
        name="layer",
    )(places, *weights, *hidden)


def gather_rows_kernel(first, places, *refs):
    out = refs[-1]
    for part, piece in enumerate(refs[:-1]):
        rows = piece.shape[0]
        out[pl.ds(pl.multiple_of(places[first + part] * rows, rows), rows), :] = piece[...]


def gather_rows(first, places, pieces):
    rows, columns = pieces[0].shape
    vmem = pl.BlockSpec(memory_space=pltpu.VMEM)
    return pl.pallas_call(
        functools.partial(gather_rows_kernel, first),
        in_specs=[pl.BlockSpec(memory_space=pltpu.SMEM)] + [vmem] * len(pieces),
        out_specs=vmem,
        out_shape=jax.ShapeDtypeStruct((rows * len(pieces), columns), pieces[0].dtype),
        compiler_params=pltpu.CompilerParams(vmem_limit_bytes=SMALL_VMEM),
        name="gather_rows",
    )(places, *pieces)


def body(sources, adjacency, target_block, source_block, slot_counts, weight):
    blks, subs, feats = (lax.axis_size(axis) for axis in ("blk", "sub", "feat"))
    blk, sub, feat = (lax.axis_index(axis) for axis in ("blk", "sub", "feat"))
    pieces = [
        forward(blk, part, blks) * subs + forward(sub, step, subs)
        for step in range(subs)
        for part in range(blks)
    ]
    turns = list(range(feats - 1, 0, -1))
    ahead = [forward(feat, step, feats) for step in [0] + turns]
    behind = [backward(feat, step, feats) for step in [0] + turns]
    places = jnp.stack(pieces + ahead + behind + [sub]).astype(jnp.int32)
    at_ahead, at_behind = len(pieces), len(pieces) + feats

    def exchange(parts):
        return [parts[0]] + [send(part, "feat", step) for part, step in zip(parts[1:], turns)]

    far, near = [blks - 1], list(range(blks - 2, 0, -1))
    other = [blks + part for part in range(blks)]
    calls = [
        [other[part] for part in far], far, [other[part] for part in near], [other[0]] + near, [0], []
    ]
    plan, held, tiles = make_plan(
        target_block, source_block, slot_counts, places, sources, adjacency, calls[0]
    )
    share = None

    def local(number, after):
        nonlocal tiles, share
        turn, now, *_ = lax.optimization_barrier((plan, tiles, *after))
        taken = () if number else (places, weight, weight.shape[0] // subs)
        made, tiles, last = products(
            held, adjacency, now, turn, calls[number], calls[number + 1], blks, taken
        )
        share = last if taken else share
        return made

    others = {}
    away = local(0, [])
    shares = [fetch(share, "feat", step) for step in reversed(turns)]
    arrived = [send(value, "sub", 1) for value in away]
    kept = local(1, away)
    sums = list(pair_sum(kept, arrived))
    others.update((part, send(value, "blk", part)) for part, value in zip(far, sums))
    away = local(2, sums)
    arrived = [send(value, "sub", 1) for value in away]
    last, *kept = local(3, away)
    sums = list(pair_sum(kept, arrived))
    others.update((part, send(value, "blk", part)) for part, value in zip(near, sums))
    (kept,) = local(4, sums)
    kept, shares = lax.optimization_barrier((kept, shares))
    dealt = deal(feats, at_ahead, places, kept, [send(last, "sub", 1)] + [others[part] for part in range(1, blks)])
    dealt, shares = lax.optimization_barrier((dealt, shares))
    hidden = exchange(dealt)
    weights = [weight]
    for part in reversed(shares):
        weights += [part, send(part, "sub", 1)]
    outs = layer(at_behind, places, hidden, weights)
    return gather_rows(at_behind, places, exchange(outs))


def solution(mesh):
    return jax.shard_map(
        body,
        mesh=mesh,
        in_specs=(
            P(("blk", "sub"), "feat"),
            P(("blk", "sub"), None, None, None, None),
            P(("blk", "sub"), None, None),
            P(("blk", "sub"), None, None),
            P(("blk", "sub"), None),
            P(None, "feat"),
        ),
        out_specs=P(("blk", "sub"), "feat"),
        check_vma=False,
    )
```
